32 devices in a mesh: ctx: 4 (over z), chan: 8 (over y, x, core).
Axes of the slice: x: 2, y: 2, z: 4, core: 2. Of those that a mesh axis runs over, the one named last changes fastest.
Arguments:
- tokens: bfloat16 [8192, 4096], P(('ctx', 'chan')), may hold values from -6 to 6
- in_weight: bfloat16 [3, 4096, 4096], P(None, None, 'chan'), may hold values from -0.09375 to 0.09375
- short_weight: float32 [3, 3, 4096], P(None, None, 'chan'), may hold values from -3 to 3
- decay_rate: float32 [16, 4096], P(None, 'chan'), may hold values from 2.4414063e-05 to 0.0333333333
- residue: float32 [16, 4096], P(None, 'chan'), may hold values from -1.5 to 1.5
- skip_gain: float32 [4096], P('chan'), may hold values from -4 to 4
- out_weight: bfloat16 [4096, 4096], P('chan'), may hold values from -0.09375 to 0.09375
Outputs:
- block_out: bfloat16 [8192, 4096], P(('ctx', 'chan'))
The draws below stay inside these ranges and needn't reach their ends.
All inputs are finite; a program needn't handle non-finite values.
Results may differ from the reference program's by a relative error of at most 0.02.
Values may be sent and summed in bfloat16 or wider, within the bound.
A program may use at most 192 MiB of HBM per device.

```python
import math
import jax
import jax.numpy as jnp
from jax import lax

D = 4096
MODES = 16
TAPS = 3
GROUP = 512
SEQ = 8192


def draw_decay_rate(key, part):
    slow_key = jax.random.fold_in(key, 11)
    low_key = jax.random.fold_in(key, 12)
    high_key = jax.random.fold_in(key, 13)
    share = 0.5
    slow_mask = jax.random.uniform(slow_key, (MODES, D), jnp.float32) < share
    slow_log = jax.random.uniform(low_key, (MODES, D), jnp.float32, math.log(0.2 / SEQ), math.log(2.0 / SEQ))
    fast_log = jax.random.uniform(high_key, (MODES, D), jnp.float32, math.log(1.0 / 50.0), math.log(1.0 / 30.0))
    return jnp.exp(jnp.where(slow_mask, slow_log, fast_log)).astype(jnp.float32)


def steps_of(stream_key, extent, cuts, least, high):
    factor_of = 1.0
    for axis_at, blocks in cuts:
        heights = jax.random.uniform(jax.random.fold_in(jax.random.fold_in(stream_key, 6), axis_at), (blocks,), jnp.float32, least / len(cuts), high / len(cuts))
        factor_of = factor_of * jnp.repeat(jnp.exp(heights), extent[axis_at] // blocks).reshape((-1,) + (1,) * (len(extent) - 1 - axis_at))
    return factor_of


def noise(stream_key, dims, spread, reach, pieces=(), kind=jnp.bfloat16):
    values = jax.random.normal(stream_key, dims, jnp.float32) * spread
    if len(pieces) > 0:
        values = steps_of(stream_key, dims, pieces, -0.22, 0.18) * values
    return jnp.clip(values, min=-reach, max=reach).astype(kind)


def setup_inputs(seed: int = 0) -> dict:
    seeds = jax.random.split(jax.random.key(seed), 8)
    return {
        "tokens": noise(seeds[0], (SEQ, D), 1.0, 6.0, ((0, 32),)),
        "in_weight": noise(seeds[1], (3, D, D), D ** -0.5, 0.09375, ((2, 8),)),
        "short_weight": noise(seeds[2], (TAPS, 3, D), 0.6, 3.0, ((2, 8),), jnp.float32),
        "decay_rate": draw_decay_rate(jax.random.fold_in(seeds[7], 71), 0),
        "residue": noise(seeds[4], (MODES, D), 0.25, 1.5, ((1, 8),), jnp.float32),
        "skip_gain": noise(seeds[5], (D,), 1.0, 4.0, ((0, 8),), jnp.float32),
        "out_weight": noise(seeds[6], (D, D), D ** -0.5, 0.09375, ((0, 8),)),
    }


def reference(tokens, in_weight, short_weight, decay_rate, residue, skip_gain, out_weight):
    projected = jnp.stack([jnp.dot(tokens, in_weight[kind], preferred_element_type=jnp.float32) for kind in range(3)], 1).astype(jnp.bfloat16)
    padded = jnp.concatenate([jnp.zeros((TAPS - 1, 3, D), jnp.bfloat16), projected], 0)
    features = jnp.zeros((SEQ, 3, D), jnp.float32)
    for offset in range(TAPS):
        features = features + short_weight[offset] * padded[TAPS - 1 - offset:TAPS - 1 - offset + SEQ].astype(jnp.float32)
    query_part = features[:, 0]
    driven = features[:, 1] * features[:, 2]
    poles = jnp.exp(-decay_rate)
    mode_gain = residue * jnp.sqrt(2.0 * decay_rate)

    def advance(carried_state, token_drive):
        carried_state = poles * carried_state + token_drive[None, :]
        return (carried_state, lax.optimization_barrier(jnp.sum(mode_gain * carried_state, 0)))
    _, long_conv = lax.scan(advance, jnp.zeros((MODES, D), jnp.float32), driven)
    gated = (query_part * (long_conv + skip_gain * driven)).astype(jnp.bfloat16)

    def add_group(running, group_idx):
        columns = lax.dynamic_slice_in_dim(gated, group_idx * GROUP, GROUP, 1)
        weight_rows = lax.dynamic_slice_in_dim(out_weight, group_idx * GROUP, GROUP, 0)
        group_part = jnp.dot(columns, weight_rows, preferred_element_type=jnp.float32).astype(jnp.bfloat16)
        group_part = lax.optimization_barrier(group_part)
        return (running + group_part.astype(jnp.float32), None)
    summed, _ = lax.scan(add_group, jnp.zeros((SEQ, D), jnp.float32), jnp.arange(D // GROUP, dtype=jnp.int32))
    return summed.astype(jnp.bfloat16)
```

```python
import functools

import jax
import jax.numpy as jnp
from jax import lax
from jax.experimental import pallas as pl
from jax.experimental.pallas import tpu as pltpu
from jax.sharding import PartitionSpec as P

MESH = pl.DeviceIdType.MESH
F32, BF16 = jnp.float32, jnp.bfloat16
LANES, SUBS, PAD = 128, 8, 8
CHAN = 8
UNROLL = 4


def kernel(
    ctxs, tokens, in_w, short_w, decay, residue, skip, out_w, out,
    grid_buf, w_buf, wo_buf, feat, excl, block_end, state, gated, gated16,
    halo_buf, load_sem, ag_send, ag_recv, halo_send, halo_recv, st_send, st_recv,
    cp_send, cp_recv, link_send, link_recv, credit, out_sem,
):
    ctx, me = lax.axis_index("ctx"), lax.axis_index("chan")
    core, xpos, ypos = me % 2, (me // 2) % 2, me // 4
    to_core, to_x, to_y = 1 - 2 * core, 2 - 4 * xpos, 4 - 8 * ypos
    cp, xp, yp = me + to_core, me + to_x, me + to_y
    diag = me + to_x + to_y
    rows, width = tokens.shape
    half = rows // 2
    tiles = in_w.shape[2] // LANES
    modes = decay.shape[0]
    seq_rows = rows * CHAN
    step_rows = rows // SUBS
    top, low = pl.ds(0, half), pl.ds(half, half)

    def send(src, dst, send_sem, recv_sem, chan=None, to_ctx=None):
        where = {"chan": chan} if to_ctx is None else {"ctx": to_ctx}
        return pltpu.make_async_remote_copy(
            src_ref=src, dst_ref=dst, send_sem=send_sem, recv_sem=recv_sem,
            device_id=where, device_id_type=MESH,
        )

    barrier = pltpu.get_barrier_semaphore()
    for partner in (cp, xp, yp):
        pl.semaphore_signal(barrier, inc=1, device_id={"chan": partner}, device_id_type=MESH)
    for off in range(1, ctxs):
        pl.semaphore_signal(
            barrier, inc=1, device_id={"ctx": (ctx + off) % ctxs}, device_id_type=MESH
        )

    loads = [pltpu.make_async_copy(tokens, grid_buf.at[me], load_sem.at[0])]
    loads += [
        pltpu.make_async_copy(in_w.at[j], w_buf.at[j], load_sem.at[1 + j]) for j in range(3)
    ]
    loads += [pltpu.make_async_copy(out_w, wo_buf, load_sem.at[4])]
    for load in loads:
        load.start()
    pl.semaphore_wait(barrier, 3 + ctxs - 1)

    def hop(i, block, part, to, src=None):
        src = grid_buf.at[block, part] if src is None else src
        return send(src, grid_buf.at[block, part], ag_send.at[i], ag_recv.at[i], chan=to)

    whole = pl.ds(0, rows)
    sent = [
        hop(0, me, top, xp, tokens.at[top]),
        hop(1, me, low, yp, tokens.at[low]),
        hop(2, me, whole, cp, tokens),
        hop(3, me, low, xp, tokens.at[low]),
        hop(4, me, top, yp, tokens.at[top]),
    ]
    for copy in sent:
        copy.start()

    def forward(i, block, part, to):
        copy = hop(i, block, part, to)
        copy.start()
        sent.append(copy)

    def arrived(i, block, part):
        hop(i, block, part, cp).wait_recv()

    def project(block):
        start = pl.multiple_of(PAD + block * rows, SUBS)

        def kind(j, _):
            made = jnp.dot(grid_buf[block], w_buf[j], preferred_element_type=F32)
            made = made.astype(BF16).astype(F32)
            for l in range(tiles):
                feat[j * tiles + l, pl.ds(start, rows), :] = made[:, l * LANES:(l + 1) * LANES]
            return 0

        lax.fori_loop(0, 3, kind, 0)

    for load in loads[:4]:
        load.wait()
    project(me)
    arrived(2, cp, whole)
    project(cp)
    arrived(0, xp, top)
    forward(5, xp, top, yp)
    forward(7, xp, top, cp)
    arrived(1, yp, low)
    forward(6, yp, low, xp)
    forward(8, yp, low, cp)
    arrived(3, xp, low)
    forward(9, xp, low, cp)
    arrived(4, yp, top)
    forward(10, yp, top, cp)
    project(xp)
    project(yp)
    arrived(7, cp + to_x, top)
    arrived(9, cp + to_x, low)
    project(cp + to_x)
    arrived(8, cp + to_y, low)
    arrived(10, cp + to_y, top)
    project(cp + to_y)
    arrived(5, diag, top)
    forward(11, diag, top, cp)
    arrived(6, diag, low)
    forward(12, diag, low, cp)
    project(diag)
    arrived(11, diag + to_core, top)
    arrived(12, diag + to_core, low)
    project(diag + to_core)

    tail = pl.ds(PAD + seq_rows - PAD, PAD)
    halo_buf[...] = feat[:, tail, :]
    halo = send(
        halo_buf, feat.at[:, pl.ds(0, PAD)], halo_send, halo_recv, to_ctx=(ctx + 1) % ctxs
    )

    @pl.when(ctx < ctxs - 1)
    def _():
        halo.start()

    for copy in sent:
        copy.wait_send()
    for partner in (cp, xp, yp):
        pl.semaphore_signal(credit, inc=1, device_id={"chan": partner}, device_id_type=MESH)

    def lanes_of(l):
        return pl.ds(pl.multiple_of(l * LANES, LANES), LANES)

    sub = lax.broadcasted_iota(jnp.int32, (modes, SUBS, LANES), 1)
    wide = (modes, SUBS, LANES)

    def first_pass(block):
        base = PAD + block * rows

        def tile(l, _):
            rate = jnp.broadcast_to(decay[:, :, lanes_of(l)], wide)
            pole = jnp.exp(-rate)
            taps = [
                [jnp.broadcast_to(short_w[k, j:j + 1, lanes_of(l)], (SUBS, LANES)) for j in range(3)]
                for k in range(3)
            ]

            def at(i):
                return pl.ds(base + i, SUBS, step_rows)

            def steps(it, carry):
                s, last, before = carry
                for u in range(UNROLL):
                    i = it * UNROLL + u
                    now = [feat[j * tiles + l, at(i), :] for j in range(3)]
                    made = [
                        taps[0][j] * now[j] + taps[1][j] * last[j] + taps[2][j] * before[j]
                        for j in range(3)
                    ]
                    driven = made[1] * made[2]
                    feat[l, at(i), :] = made[0]
                    feat[tiles + l, at(i), :] = driven
                    s = pole * s + driven[None]
                    last, before = now, last
                return s, last, before

            s, _, _ = lax.fori_loop(
                0, step_rows // UNROLL, steps,
                (
                    jnp.zeros(wide, F32),
                    [feat[j * tiles + l, at(-1), :] for j in range(3)],
                    [feat[j * tiles + l, at(-2), :] for j in range(3)],
                ),
            )
            for shift in (1, 2, 4):
                fade = jnp.exp(-rate * float(step_rows * shift))
                s = s + jnp.where(sub >= shift, pltpu.roll(s, shift, 1) * fade, 0.0)
            excl[block, l] = jnp.where(sub >= 1, pltpu.roll(s, 1, 1), 0.0)
            block_end[block, l] = s[:, SUBS - 1:SUBS, :]
            return 0

        lax.fori_loop(0, tiles, tile, 0)

    def backwards(i, _):
        first_pass(CHAN - 1 - i)
        return 0

    lax.fori_loop(0, CHAN - 1, backwards, 0)

    @pl.when(ctx == 0)
    def _():
        feat[:, 0:PAD, :] = jnp.zeros((3 * tiles, PAD, LANES), F32)

    @pl.when(ctx > 0)
    def _():
        halo.wait_recv()

    @pl.when(ctx < ctxs - 1)
    def _():
        halo.wait_send()

    first_pass(0)

    def own_state(l, _):
        fade = jnp.exp(-decay[:, :, lanes_of(l)] * float(rows))
        total = block_end[0, l]
        for block in range(1, CHAN):
            total = fade * total + block_end[block, l]
        state[ctx, l] = total
        return 0

    lax.fori_loop(0, tiles, own_state, 0)
    state_copies = []
    for off in range(1, ctxs):
        copy = send(
            state.at[ctx], state.at[ctx], st_send.at[off], st_recv.at[off],
            to_ctx=(ctx + off) % ctxs,
        )
        copy.start()
        state_copies.append(copy)
    for off in range(1, ctxs):
        source = (ctx + ctxs - off) % ctxs
        send(
            state.at[source], state.at[source], st_send.at[off], st_recv.at[off], to_ctx=source
        ).wait_recv()

    def enter(l, _):
        rate = decay[:, :, lanes_of(l)]
        s = jnp.zeros((modes, 1, LANES), F32)
        for off in range(1, ctxs):
            source = (ctx + ctxs - off) % ctxs
            known = jnp.where(ctx >= off, 1.0, 0.0).astype(F32)
            s = s + known * jnp.exp(-rate * float(seq_rows * (off - 1))) * state[source, l]
        fade = jnp.exp(-rate * float(rows))
        inner = jnp.exp(-jnp.broadcast_to(rate, wide) * (sub * step_rows).astype(F32))
        for block in range(CHAN):
            excl[block, l] = excl[block, l] + inner * s
            s = fade * s + block_end[block, l]
        return 0

    lax.fori_loop(0, tiles, enter, 0)

    def gate(block):
        base = PAD + block * rows

        def tile(l, _):
            rate = jnp.broadcast_to(decay[:, :, lanes_of(l)], wide)
            pole = jnp.exp(-rate)
            gain = jnp.broadcast_to(residue[:, :, lanes_of(l)], wide) * jnp.sqrt(2.0 * rate)
            direct = jnp.broadcast_to(skip[:, lanes_of(l)], (SUBS, LANES))

            def steps(it, s):
                for u in range(UNROLL):
                    i = it * UNROLL + u
                    at = pl.ds(base + i, SUBS, step_rows)
                    driven = feat[tiles + l, at, :]
                    s = pole * s + driven[None]
                    y = jnp.sum(gain * s, axis=0) + direct * driven
                    gated[l, pl.ds(i, SUBS, step_rows), :] = feat[l, at, :] * y
                return s

            lax.fori_loop(0, step_rows // UNROLL, steps, excl[block, l])
            return 0

        lax.fori_loop(0, tiles, tile, 0)
        for l in range(tiles):
            gated16[:, l * LANES:(l + 1) * LANES] = gated[l].astype(BF16)

    cut = 512

    def over_width(body):
        def one(t, _):
            body(pl.ds(pl.multiple_of(t * cut, cut), cut))
            return 0

        lax.fori_loop(0, width // cut, one, 0)

    def multiply(slot, add):
        def body(cols):
            made = jnp.dot(gated16[...], wo_buf[:, cols], preferred_element_type=F32).astype(BF16)
            if add:
                made = (grid_buf[slot, :, cols].astype(F32) + made.astype(F32)).astype(BF16)
            grid_buf[slot, :, cols] = made

        over_width(body)

    loads[4].wait()
    pl.semaphore_wait(credit, 3)

    def link(i, src_slot, dst_slot, part, to):
        return send(
            grid_buf.at[src_slot, part], grid_buf.at[dst_slot, part],
            link_send.at[i], link_recv.at[i], chan=to,
        )

    linked = []

    def go(*what):
        copy = link(*what)
        copy.start()
        linked.append(copy)

    to_other = []
    for i, mine in enumerate((diag, xp, yp, me)):
        stage = 7 + i % 2
        gate(mine + to_core)
        if i >= 2:
            to_other[i - 2].wait_send()
        multiply(stage, False)
        copy = send(
            grid_buf.at[stage], grid_buf.at[i], cp_send.at[i], cp_recv.at[i], chan=cp
        )
        copy.start()
        to_other.append(copy)
        gate(mine)
        copy.wait_recv()
        multiply(i, True)
        if i == 0:
            go(0, 0, 4, top, xp)
            go(1, 0, 4, low, yp)
        if i == 1:
            go(2, 1, 5, top, xp)
        if i == 2:
            go(3, 2, 6, low, yp)

    def join(dst, part, *slots):
        def body(cols):
            total = grid_buf[slots[0], part, cols].astype(F32)
            for slot in slots[1:]:
                total = total + grid_buf[slot, part, cols].astype(F32)
            grid_buf[dst, part, cols] = total.astype(BF16)

        over_width(body)

    link(1, 0, 4, low, yp).wait_recv()
    join(1, low, 1, 4)
    go(4, 1, 5, low, xp)
    link(0, 0, 4, top, xp).wait_recv()
    join(2, top, 2, 4)
    go(5, 2, 6, top, yp)
    for copy in to_other[2:]:
        copy.wait_send()
    results = []
    for h, part, early, late in ((0, top, (2, 5), (5, 6)), (1, low, (3, 6), (4, 5))):
        link(early[0], 0, early[1], part, xp).wait_recv()
        link(late[0], 0, late[1], part, xp).wait_recv()
        join(7, part, 3, 5, 6)
        result = pltpu.make_async_copy(grid_buf.at[7, part], out.at[part], out_sem.at[h])
        result.start()
        results.append(result)
    for copy in linked:
        copy.wait_send()
    for copy in state_copies:
        copy.wait_send()
    for result in results:
        result.wait()


def local(ctxs, tokens, in_weight, short_weight, decay_rate, residue, skip_gain, out_weight):
    rows, width = tokens.shape
    chans = in_weight.shape[2]
    modes = decay_rate.shape[0]
    tiles = chans // LANES
    seq_rows = rows * CHAN
    any_spec = pl.BlockSpec(memory_space=pl.ANY)
    vmem = pl.BlockSpec(memory_space=pltpu.VMEM)
    dma = pltpu.SemaphoreType.DMA
    return pl.pallas_call(
        functools.partial(kernel, ctxs),
        out_shape=jax.ShapeDtypeStruct((rows, width), BF16),
        in_specs=[any_spec, any_spec, vmem, vmem, vmem, vmem, any_spec],
        out_specs=any_spec,
        scratch_shapes=[
            pltpu.VMEM((CHAN + 1, rows, width), BF16),
            pltpu.VMEM(in_weight.shape, BF16),
            pltpu.VMEM(out_weight.shape, BF16),
            pltpu.VMEM((3 * tiles, PAD + seq_rows, LANES), F32),
            pltpu.VMEM((CHAN, tiles, modes, SUBS, LANES), F32),
            pltpu.VMEM((CHAN, tiles, modes, 1, LANES), F32),
            pltpu.VMEM((ctxs, tiles, modes, 1, LANES), F32),
            pltpu.VMEM((tiles, rows, LANES), F32),
            pltpu.VMEM((rows, chans), BF16),
            pltpu.VMEM((3 * tiles, PAD, LANES), F32),
            dma((5,)), dma((13,)), dma((13,)), dma, dma, dma((ctxs,)), dma((ctxs,)),
            dma((4,)), dma((4,)), dma((6,)), dma((6,)),
            pltpu.SemaphoreType.REGULAR, dma((2,)),
        ],
        compiler_params=pltpu.CompilerParams(
            collective_id=0, has_side_effects=True, vmem_limit_bytes=62 * 2**20
        ),
        cost_estimate=pl.CostEstimate(
            flops=2 * seq_rows * width * 4 * chans,
            bytes_accessed=2 * 4 * width * chans + 4 * rows * width,
            transcendentals=0,
        ),
    )(
        tokens, in_weight, short_weight,
        decay_rate.reshape(modes, 1, chans), residue.reshape(modes, 1, chans),
        skip_gain.reshape(1, chans), out_weight,
    )


HIGH = lax.Precision.HIGHEST


def from_behind(array, axis, by):
    size = lax.axis_size(axis)
    pairs = [(i, i + by) for i in range(size) if 0 <= i + by < size]
    return lax.ppermute(array, axis, pairs)


def prefix(array, axis, combine, identity):
    size, mine = (lax.axis_size(axis), lax.axis_index(axis))
    everything = jax.tree.map(
        lambda part, kind: lax.all_gather(part.astype(kind), axis),
        array,
        (jnp.bfloat16, jnp.bfloat16),
    )
    start = jax.tree.map(
        lambda part, zero: jnp.broadcast_to(jnp.asarray(zero, part.dtype), part.shape),
        array,
        identity,
    )

    def lap(k, before):
        reached = k < mine
        new = combine(
            before, jax.tree.map(lambda part, own: part[k].astype(own.dtype), everything, array)
        )
        return jax.tree.map(lambda a, b: jnp.where(reached, a, b), new, before)

    return lax.fori_loop(0, size, lap, start)


def merge_states(earlier, latter):
    return (earlier[0] * latter[0], latter[0] * earlier[1] + latter[1])


def general(tokens, in_weight, short_weight, decay_rate, residue, skip_gain, out_weight):
    group_chans = in_weight.shape[2]
    filter_taps = short_weight.shape[0]
    projected = jnp.einsum(
        "ld,jdc->ljc",
        lax.all_gather(tokens, "chan", axis=0, tiled=True),
        in_weight,
        preferred_element_type=jnp.float32,
    ).astype(jnp.bfloat16)
    seq_rows = projected.shape[0]
    earlier_rows = from_behind(projected[seq_rows - (filter_taps - 1) :], "ctx", 1)
    padded = jnp.concatenate([earlier_rows, projected], 0)
    features = jnp.zeros((seq_rows, 3, group_chans), jnp.float32)
    for offset in range(filter_taps):
        features = features + short_weight[offset] * padded[
            filter_taps - 1 - offset : filter_taps - 1 - offset + seq_rows
        ].astype(jnp.float32)
    query_part = features[:, 0]
    driven = features[:, 1] * features[:, 2]
    mode_gain = residue * jnp.sqrt(2.0 * decay_rate)
    block_len = 128
    block_count = seq_rows // block_len
    lag_steps = jnp.arange(block_len, dtype=jnp.float32)
    decay_table = jnp.exp(-decay_rate[:, None, :] * lag_steps[None, :, None])
    lag_filter = jnp.sum(decay_table * mode_gain[:, None, :], 0)
    row_idx = jnp.arange(block_len)[:, None]
    col_idx = jnp.arange(block_len)[None, :]
    lag_index = jnp.maximum(row_idx - col_idx, 0)
    toeplitz = jnp.where(
        (row_idx >= col_idx)[:, :, None], jnp.take(lag_filter, lag_index, axis=0), 0.0
    )
    blocked = driven.reshape(block_count, block_len, group_chans)
    inner_part = jnp.einsum("ijc,bjc->bic", toeplitz, blocked, precision=HIGH)
    block_ends = jnp.einsum("rjc,bjc->brc", decay_table[:, ::-1, :], blocked, precision=HIGH)
    block_pos = jnp.arange(block_count, dtype=jnp.float32)
    block_gap = block_pos[:, None] - 1.0 - block_pos[None, :]
    block_mix = jnp.where(
        (block_gap >= 0.0)[:, :, None, None],
        jnp.exp(
            -decay_rate[None, None] * block_len * jnp.maximum(block_gap, 0.0)[:, :, None, None]
        ),
        0.0,
    )
    before = jnp.einsum("xyrc,yrc->xrc", block_mix, block_ends, precision=HIGH)
    tail_weight = jnp.exp(
        -decay_rate[None] * block_len * (block_count - 1.0 - block_pos)[:, None, None]
    )
    own_state = jnp.sum(tail_weight * block_ends, 0)
    device_span = jnp.exp(-decay_rate * seq_rows)
    identity = (jnp.ones_like(device_span), jnp.zeros_like(own_state))
    entering = prefix((device_span, own_state), "ctx", merge_states, identity)[1]
    before = (
        before + jnp.exp(-decay_rate[None] * block_len * block_pos[:, None, None]) * entering[None]
    )
    rise_table = mode_gain[:, None, :] * decay_table * jnp.exp(-decay_rate)[:, None, :]
    carried = jnp.einsum("ric,brc->bic", rise_table, before, precision=HIGH)
    long_conv = (inner_part + carried).reshape(seq_rows, group_chans)
    gated = (query_part * (long_conv + skip_gain * driven)).astype(jnp.bfloat16)
    rounded = jnp.dot(gated, out_weight, preferred_element_type=jnp.float32).astype(jnp.bfloat16)
    return lax.psum_scatter(
        lax.optimization_barrier(rounded).astype(jnp.float32).astype(jnp.bfloat16),
        "chan",
        scatter_dimension=0,
        tiled=True,
    )


def solution(mesh):
    square = mesh.shape["chan"] == CHAN
    return jax.shard_map(
        functools.partial(local, mesh.shape["ctx"]) if square else general,
        mesh=mesh,
        in_specs=(
            P(("ctx", "chan"), None),
            P(None, None, "chan"),
            P(None, None, "chan"),
            P(None, "chan"),
            P(None, "chan"),
            P("chan"),
            P("chan", None),
        ),
        out_specs=P(("ctx", "chan"), None),
        check_vma=False,
    )
```

```python
import functools

import jax
import jax.numpy as jnp
from jax import lax
from jax.experimental import pallas as pl
from jax.experimental.pallas import tpu as pltpu
from jax.sharding import PartitionSpec as P

MESH = pl.DeviceIdType.MESH
F32, BF16 = jnp.float32, jnp.bfloat16
LANES, SUBS, PAD = 128, 8, 8
CHAN = 8
UNROLL = 4


def kernel(
    ctxs, tokens, in_w, short_w, decay_in, residue_in, skip, out_w, out,
    grid_buf, w_buf, wo_buf, feat, excl, block_end, state, gated, gated16,
    head, edge, decay, residue, load_sem, ag_send, ag_recv, halo_send, halo_recv, st_send, st_recv,
    cp_send, cp_recv, link_send, link_recv, credit, out_sem,
):
    ctx, me = lax.axis_index("ctx"), lax.axis_index("chan")
    core, xpos, ypos = me % 2, (me // 2) % 2, me // 4
    to_core, to_x, to_y = 1 - 2 * core, 2 - 4 * xpos, 4 - 8 * ypos
    cp, xp, yp = me + to_core, me + to_x, me + to_y
    diag = me + to_x + to_y
    rows, width = tokens.shape
    half = rows // 2
    tiles = in_w.shape[2] // LANES
    modes = decay_in.shape[0]
    seq_rows = rows * CHAN
    step_rows = rows // SUBS
    top, low = pl.ds(0, half), pl.ds(half, half)

    def send(src, dst, send_sem, recv_sem, chan=None, to_ctx=None):
        where = {"chan": chan} if to_ctx is None else {"ctx": to_ctx}
        return pltpu.make_async_remote_copy(
            src_ref=src, dst_ref=dst, send_sem=send_sem, recv_sem=recv_sem,
            device_id=where, device_id_type=MESH,
        )

    barrier = pltpu.get_barrier_semaphore()
    for partner in (cp, xp, yp):
        pl.semaphore_signal(barrier, inc=1, device_id={"chan": partner}, device_id_type=MESH)
    for off in range(1, ctxs):
        pl.semaphore_signal(
            barrier, inc=1, device_id={"ctx": (ctx + off) % ctxs}, device_id_type=MESH
        )

    loads = [pltpu.make_async_copy(tokens, grid_buf.at[me], load_sem.at[0])]
    loads += [
        pltpu.make_async_copy(in_w.at[j], w_buf.at[j], load_sem.at[1 + j]) for j in range(3)
    ]
    loads += [pltpu.make_async_copy(out_w, wo_buf, load_sem.at[4])]
    for load in loads:
        load.start()
    pl.semaphore_wait(barrier, 3 + ctxs - 1)

    def hop(i, block, part, to, src=None):
        src = grid_buf.at[block, part] if src is None else src
        return send(src, grid_buf.at[block, part], ag_send.at[i], ag_recv.at[i], chan=to)

    whole = pl.ds(0, rows)
    sent = [
        hop(0, me, top, xp, tokens.at[top]),
        hop(1, me, low, yp, tokens.at[low]),
        hop(2, me, whole, cp, tokens),
        hop(3, me, low, xp, tokens.at[low]),
        hop(4, me, top, yp, tokens.at[top]),
    ]
    for copy in sent:
        copy.start()

    def forward(i, block, part, to):
        copy = hop(i, block, part, to)
        copy.start()
        sent.append(copy)

    def arrived(i, block, part):
        hop(i, block, part, cp).wait_recv()

    def project(block):
        start = pl.multiple_of(PAD + block * rows, SUBS)

        def kind(j, _):
            made = jnp.dot(grid_buf[block], w_buf[j], preferred_element_type=F32)
            made = made.astype(BF16).astype(F32)
            for l in range(tiles):
                feat[j * tiles + l, pl.ds(start, rows), :] = made[:, l * LANES:(l + 1) * LANES]
            return 0

        lax.fori_loop(0, 3, kind, 0)
        head[block] = feat[:, pl.ds(start, PAD), :]
        edge[block + 1] = feat[:, pl.ds(pl.multiple_of(start + rows - PAD, SUBS), PAD), :]

    def lanes_of(l):
        return pl.ds(pl.multiple_of(l * LANES, LANES), LANES)

    sub = lax.broadcasted_iota(jnp.int32, (modes, SUBS, LANES), 1)
    sub2 = lax.broadcasted_iota(jnp.int32, (SUBS, LANES), 0)
    wide = (modes, SUBS, LANES)

    def first_pass(block):
        base = PAD + block * rows

        def tile(l, _):
            rate = jnp.broadcast_to(decay[:, :, lanes_of(l)], wide)
            pole = jnp.exp(-rate)
            taps = [
                [jnp.broadcast_to(short_w[k, j:j + 1, lanes_of(l)], (SUBS, LANES)) for j in range(3)]
                for k in range(3)
            ]

            def at(i):
                return pl.ds(base + i, SUBS, step_rows)

            def steps(it, carry):
                s, last, before = carry
                for u in range(UNROLL):
                    i = it * UNROLL + u
                    now = [feat[j * tiles + l, at(i), :] for j in range(3)]
                    made = [
                        taps[0][j] * now[j] + taps[1][j] * last[j] + taps[2][j] * before[j]
                        for j in range(3)
                    ]
                    driven = made[1] * made[2]
                    feat[l, at(i), :] = made[0]
                    feat[tiles + l, at(i), :] = driven
                    s = pole * s + driven[None]
                    last, before = now, last
                return s, last, before

            there = (sub2 > 0) | (block % 2 == 1)

            def ahead(i):
                return [
                    jnp.where(there, feat[j * tiles + l, at(i), :], 0.0) for j in range(3)
                ]

            s, _, _ = lax.fori_loop(
                0, step_rows // UNROLL, steps, (jnp.zeros(wide, F32), ahead(-1), ahead(-2))
            )
            for shift in (1, 2, 4):
                fade = jnp.exp(-rate * float(step_rows * shift))
                s = s + jnp.where(sub >= shift, pltpu.roll(s, shift, 1) * fade, 0.0)
            excl[block, l] = jnp.where(sub >= 1, pltpu.roll(s, 1, 1), 0.0)
            block_end[block, l] = s[:, SUBS - 1:SUBS, :]
            return 0

        lax.fori_loop(0, tiles, tile, 0)

    def first_rows(block):
        start = pl.ds(pl.multiple_of(PAD + block * rows, SUBS), SUBS)

        def tile(l, _):
            made = []
            for j in range(3):
                own, prior = head[block, j * tiles + l], edge[block, j * tiles + l]
                last = jnp.where(sub2 < 1, pltpu.roll(prior, 1, 0), pltpu.roll(own, 1, 0))
                before = jnp.where(sub2 < 2, pltpu.roll(prior, 2, 0), pltpu.roll(own, 2, 0))
                tap = [
                    jnp.broadcast_to(short_w[k, j:j + 1, lanes_of(l)], (SUBS, LANES))
                    for k in range(3)
                ]
                made.append(tap[0] * own + tap[1] * last + tap[2] * before)
            feat[l, start, :] = jnp.where(sub2 < 2, made[0], feat[l, start, :])
            old = feat[tiles + l, start, :]
            new = jnp.where(sub2 < 2, made[1] * made[2], old)
            feat[tiles + l, start, :] = new
            more = new - old
            zeroth, first = more[0:1, :][None], more[1:2, :][None]
            rate = decay[:, :, lanes_of(l)]
            up = jnp.exp(rate)
            lag = jnp.maximum(sub * step_rows - 1, 0).astype(F32)
            fade = jnp.exp(-jnp.broadcast_to(rate, wide) * lag)
            add = fade * (zeroth + jnp.broadcast_to(up * first, wide))
            excl[block, l] = excl[block, l] + jnp.where(sub >= 1, add, 0.0)
            block_end[block, l] = block_end[block, l] + jnp.exp(-rate * float(rows - 1)) * (
                zeroth + up * first
            )
            return 0

        lax.fori_loop(0, tiles, tile, 0)

    for r in range(modes):
        decay[r] = decay_in[r:r + 1, :]
        residue[r] = residue_in[r:r + 1, :]
    for load in loads[:4]:
        load.wait()
    project(me)
    arrived(2, cp, whole)
    project(cp)
    first_pass(me - core + 1)
    first_pass(me - core)
    arrived(0, xp, top)
    forward(5, xp, top, yp)
    forward(7, xp, top, cp)
    arrived(1, yp, low)
    forward(6, yp, low, xp)
    forward(8, yp, low, cp)
    arrived(3, xp, low)
    forward(9, xp, low, cp)
    arrived(4, yp, top)
    forward(10, yp, top, cp)
    project(xp)
    project(yp)
    arrived(7, cp + to_x, top)
    arrived(9, cp + to_x, low)
    project(cp + to_x)
    arrived(8, cp + to_y, low)
    arrived(10, cp + to_y, top)
    project(cp + to_y)
    for even in (xp - core, yp - core):
        first_pass(even + 1)
        first_pass(even)
    arrived(5, diag, top)
    forward(11, diag, top, cp)
    arrived(6, diag, low)
    forward(12, diag, low, cp)
    project(diag)
    arrived(11, diag + to_core, top)
    arrived(12, diag + to_core, low)
    project(diag + to_core)

    halo = send(
        edge.at[CHAN], edge.at[0], halo_send, halo_recv, to_ctx=(ctx + 1) % ctxs
    )

    @pl.when(ctx < ctxs - 1)
    def _():
        halo.start()

    first_pass(diag - core + 1)
    first_pass(diag - core)
    for copy in sent:
        copy.wait_send()
    for partner in (cp, xp, yp):
        pl.semaphore_signal(credit, inc=1, device_id={"chan": partner}, device_id_type=MESH)

    def fix(half_block, _):
        first_rows(2 * half_block)
        return 0

    lax.fori_loop(1, CHAN // 2, fix, 0)

    @pl.when(ctx == 0)
    def _():
        edge[0] = jnp.zeros((3 * tiles, PAD, LANES), F32)

    @pl.when(ctx > 0)
    def _():
        halo.wait_recv()

    @pl.when(ctx < ctxs - 1)
    def _():
        halo.wait_send()

    first_rows(0)

    def own_state(l, _):
        fade = jnp.exp(-decay[:, :, lanes_of(l)] * float(rows))
        total = block_end[0, l]
        for block in range(1, CHAN):
            total = fade * total + block_end[block, l]
        state[ctx, l] = total
        return 0

    lax.fori_loop(0, tiles, own_state, 0)
    state_copies = []
    for off in range(1, ctxs):
        copy = send(
            state.at[ctx], state.at[ctx], st_send.at[off], st_recv.at[off],
            to_ctx=(ctx + off) % ctxs,
        )
        copy.start()
        state_copies.append(copy)
    for off in range(1, ctxs):
        source = (ctx + ctxs - off) % ctxs
        send(
            state.at[source], state.at[source], st_send.at[off], st_recv.at[off], to_ctx=source
        ).wait_recv()

    def enter(l, _):
        rate = decay[:, :, lanes_of(l)]
        s = jnp.zeros((modes, 1, LANES), F32)
        for off in range(1, ctxs):
            source = (ctx + ctxs - off) % ctxs
            known = jnp.where(ctx >= off, 1.0, 0.0).astype(F32)
            s = s + known * jnp.exp(-rate * float(seq_rows * (off - 1))) * state[source, l]
        fade = jnp.exp(-rate * float(rows))
        inner = jnp.exp(-jnp.broadcast_to(rate, wide) * (sub * step_rows).astype(F32))
        for block in range(CHAN):
            excl[block, l] = excl[block, l] + inner * s
            s = fade * s + block_end[block, l]
        return 0

    lax.fori_loop(0, tiles, enter, 0)

    def gate(block):
        base = PAD + block * rows

        def tile(l, _):
            rate = jnp.broadcast_to(decay[:, :, lanes_of(l)], wide)
            pole = jnp.exp(-rate)
            gain = jnp.broadcast_to(residue[:, :, lanes_of(l)], wide) * jnp.sqrt(2.0 * rate)
            direct = jnp.broadcast_to(skip[:, lanes_of(l)], (SUBS, LANES))

            def steps(it, s):
                for u in range(UNROLL):
                    i = it * UNROLL + u
                    at = pl.ds(base + i, SUBS, step_rows)
                    driven = feat[tiles + l, at, :]
                    s = pole * s + driven[None]
                    y = jnp.sum(gain * s, axis=0) + direct * driven
                    gated[l, pl.ds(i, SUBS, step_rows), :] = feat[l, at, :] * y
                return s

            lax.fori_loop(0, step_rows // UNROLL, steps, excl[block, l])
            return 0

        lax.fori_loop(0, tiles, tile, 0)
        for l in range(tiles):
            gated16[:, l * LANES:(l + 1) * LANES] = gated[l].astype(BF16)

    cut = 512

    def over_width(body):
        def one(t, _):
            body(pl.ds(pl.multiple_of(t * cut, cut), cut))
            return 0

        lax.fori_loop(0, width // cut, one, 0)

    def multiply(slot, add, part=whole):
        def body(cols):
            made = jnp.dot(gated16[part, :], wo_buf[:, cols], preferred_element_type=F32).astype(BF16)
            if add:
                made = (grid_buf[slot, part, cols].astype(F32) + made.astype(F32)).astype(BF16)
            grid_buf[slot, part, cols] = made

        over_width(body)

    loads[4].wait()
    pl.semaphore_wait(credit, 3)

    def link(i, src_slot, dst_slot, part, to):
        return send(
            grid_buf.at[src_slot, part], grid_buf.at[dst_slot, part],
            link_send.at[i], link_recv.at[i], chan=to,
        )

    linked = []

    def go(*what):
        copy = link(*what)
        copy.start()
        linked.append(copy)

    to_other = []
    for i, mine in enumerate((diag, xp, yp, me)):
        stage = 7 + i % 2
        parts = ((top, 0), (low, 4)) if i == 0 else ((whole, i),)
        gate(mine + to_core)
        if i >= 2:
            for copy in to_other[i - 2]:
                copy.wait_send()
        copies = []
        for part, sem in parts:
            multiply(stage, False, part)
            copy = send(
                grid_buf.at[stage, part], grid_buf.at[i, part],
                cp_send.at[sem], cp_recv.at[sem], chan=cp,
            )
            copy.start()
            copies.append(copy)
        to_other.append(copies)
        gate(mine)
        for copy, (part, _) in zip(copies, parts):
            copy.wait_recv()
            multiply(i, True, part)
            if i == 0 and part is top:
                go(0, 0, 4, top, xp)
            if i == 0 and part is low:
                go(1, 0, 4, low, yp)
        if i == 1:
            go(2, 1, 5, top, xp)
        if i == 2:
            go(3, 2, 6, low, yp)

    def join(dst, part, *slots):
        def body(cols):
            total = grid_buf[slots[0], part, cols].astype(F32)
            for slot in slots[1:]:
                total = total + grid_buf[slot, part, cols].astype(F32)
            grid_buf[dst, part, cols] = total.astype(BF16)

        over_width(body)

    link(1, 0, 4, low, yp).wait_recv()
    join(1, low, 1, 4)
    go(4, 1, 5, low, xp)
    link(0, 0, 4, top, xp).wait_recv()
    join(2, top, 2, 4)
    go(5, 2, 6, top, yp)
    for copies in to_other[2:]:
        for copy in copies:
            copy.wait_send()
    results = []
    for h, part, early, late in ((0, top, (2, 5), (5, 6)), (1, low, (3, 6), (4, 5))):
        link(early[0], 0, early[1], part, xp).wait_recv()
        link(late[0], 0, late[1], part, xp).wait_recv()
        join(7, part, 3, 5, 6)
        result = pltpu.make_async_copy(grid_buf.at[7, part], out.at[part], out_sem.at[h])
        result.start()
        results.append(result)
    for copy in linked:
        copy.wait_send()
    for copy in state_copies:
        copy.wait_send()
    for result in results:
        result.wait()


def local(ctxs, tokens, in_weight, short_weight, decay_rate, residue, skip_gain, out_weight):
    rows, width = tokens.shape
    chans = in_weight.shape[2]
    modes = decay_rate.shape[0]
    tiles = chans // LANES
    seq_rows = rows * CHAN
    any_spec = pl.BlockSpec(memory_space=pl.ANY)
    vmem = pl.BlockSpec(memory_space=pltpu.VMEM)
    dma = pltpu.SemaphoreType.DMA
    return pl.pallas_call(
        functools.partial(kernel, ctxs),
        out_shape=jax.ShapeDtypeStruct((rows, width), BF16),
        in_specs=[any_spec, any_spec, vmem, vmem, vmem, vmem, any_spec],
        out_specs=any_spec,
        scratch_shapes=[
            pltpu.VMEM((CHAN + 1, rows, width), BF16),
            pltpu.VMEM(in_weight.shape, BF16),
            pltpu.VMEM(out_weight.shape, BF16),
            pltpu.VMEM((3 * tiles, PAD + seq_rows, LANES), F32),
            pltpu.VMEM((CHAN, tiles, modes, SUBS, LANES), F32),
            pltpu.VMEM((CHAN, tiles, modes, 1, LANES), F32),
            pltpu.VMEM((ctxs, tiles, modes, 1, LANES), F32),
            pltpu.VMEM((tiles, rows, LANES), F32),
            pltpu.VMEM((rows, chans), BF16),
            pltpu.VMEM((CHAN, 3 * tiles, PAD, LANES), F32),
            pltpu.VMEM((CHAN + 1, 3 * tiles, PAD, LANES), F32),
            pltpu.VMEM((modes, 1, chans), F32),
            pltpu.VMEM((modes, 1, chans), F32),
            dma((5,)), dma((13,)), dma((13,)), dma, dma, dma((ctxs,)), dma((ctxs,)),
            dma((5,)), dma((5,)), dma((6,)), dma((6,)),
            pltpu.SemaphoreType.REGULAR, dma((2,)),
        ],
        compiler_params=pltpu.CompilerParams(
            collective_id=0, has_side_effects=True, vmem_limit_bytes=62 * 2**20
        ),
        cost_estimate=pl.CostEstimate(
            flops=2 * seq_rows * width * 4 * chans,
            bytes_accessed=2 * 4 * width * chans + 4 * rows * width,
            transcendentals=0,
        ),
    )(
        tokens, in_weight, short_weight,
        decay_rate, residue, skip_gain.reshape(1, chans), out_weight,
    )


HIGH = lax.Precision.HIGHEST


def from_behind(array, axis, by):
    size = lax.axis_size(axis)
    pairs = [(i, i + by) for i in range(size) if 0 <= i + by < size]
    return lax.ppermute(array, axis, pairs)


def prefix(array, axis, combine, identity):
    size, mine = (lax.axis_size(axis), lax.axis_index(axis))
    everything = jax.tree.map(
        lambda part, kind: lax.all_gather(part.astype(kind), axis),
        array,
        (jnp.bfloat16, jnp.bfloat16),
    )
    start = jax.tree.map(
        lambda part, zero: jnp.broadcast_to(jnp.asarray(zero, part.dtype), part.shape),
        array,
        identity,
    )

    def lap(k, before):
        reached = k < mine
        new = combine(
            before, jax.tree.map(lambda part, own: part[k].astype(own.dtype), everything, array)
        )
        return jax.tree.map(lambda a, b: jnp.where(reached, a, b), new, before)

    return lax.fori_loop(0, size, lap, start)


def merge_states(earlier, latter):
    return (earlier[0] * latter[0], latter[0] * earlier[1] + latter[1])


def general(tokens, in_weight, short_weight, decay_rate, residue, skip_gain, out_weight):
    group_chans = in_weight.shape[2]
    filter_taps = short_weight.shape[0]
    projected = jnp.einsum(
        "ld,jdc->ljc",
        lax.all_gather(tokens, "chan", axis=0, tiled=True),
        in_weight,
        preferred_element_type=jnp.float32,
    ).astype(jnp.bfloat16)
    seq_rows = projected.shape[0]
    earlier_rows = from_behind(projected[seq_rows - (filter_taps - 1) :], "ctx", 1)
    padded = jnp.concatenate([earlier_rows, projected], 0)
    features = jnp.zeros((seq_rows, 3, group_chans), jnp.float32)
    for offset in range(filter_taps):
        features = features + short_weight[offset] * padded[
            filter_taps - 1 - offset : filter_taps - 1 - offset + seq_rows
        ].astype(jnp.float32)
    query_part = features[:, 0]
    driven = features[:, 1] * features[:, 2]
    mode_gain = residue * jnp.sqrt(2.0 * decay_rate)
    block_len = 128
    block_count = seq_rows // block_len
    lag_steps = jnp.arange(block_len, dtype=jnp.float32)
    decay_table = jnp.exp(-decay_rate[:, None, :] * lag_steps[None, :, None])
    lag_filter = jnp.sum(decay_table * mode_gain[:, None, :], 0)
    row_idx = jnp.arange(block_len)[:, None]
    col_idx = jnp.arange(block_len)[None, :]
    lag_index = jnp.maximum(row_idx - col_idx, 0)
    toeplitz = jnp.where(
        (row_idx >= col_idx)[:, :, None], jnp.take(lag_filter, lag_index, axis=0), 0.0
    )
    blocked = driven.reshape(block_count, block_len, group_chans)
    inner_part = jnp.einsum("ijc,bjc->bic", toeplitz, blocked, precision=HIGH)
    block_ends = jnp.einsum("rjc,bjc->brc", decay_table[:, ::-1, :], blocked, precision=HIGH)
    block_pos = jnp.arange(block_count, dtype=jnp.float32)
    block_gap = block_pos[:, None] - 1.0 - block_pos[None, :]
    block_mix = jnp.where(
        (block_gap >= 0.0)[:, :, None, None],
        jnp.exp(
            -decay_rate[None, None] * block_len * jnp.maximum(block_gap, 0.0)[:, :, None, None]
        ),
        0.0,
    )
    before = jnp.einsum("xyrc,yrc->xrc", block_mix, block_ends, precision=HIGH)
    tail_weight = jnp.exp(
        -decay_rate[None] * block_len * (block_count - 1.0 - block_pos)[:, None, None]
    )
    own_state = jnp.sum(tail_weight * block_ends, 0)
    device_span = jnp.exp(-decay_rate * seq_rows)
    identity = (jnp.ones_like(device_span), jnp.zeros_like(own_state))
    entering = prefix((device_span, own_state), "ctx", merge_states, identity)[1]
    before = (
        before + jnp.exp(-decay_rate[None] * block_len * block_pos[:, None, None]) * entering[None]
    )
    rise_table = mode_gain[:, None, :] * decay_table * jnp.exp(-decay_rate)[:, None, :]
    carried = jnp.einsum("ric,brc->bic", rise_table, before, precision=HIGH)
    long_conv = (inner_part + carried).reshape(seq_rows, group_chans)
    gated = (query_part * (long_conv + skip_gain * driven)).astype(jnp.bfloat16)
    rounded = jnp.dot(gated, out_weight, preferred_element_type=jnp.float32).astype(jnp.bfloat16)
    return lax.psum_scatter(
        lax.optimization_barrier(rounded).astype(jnp.float32).astype(jnp.bfloat16),
        "chan",
        scatter_dimension=0,
        tiled=True,
    )


def solution(mesh):
    square = mesh.shape["chan"] == CHAN
    return jax.shard_map(
        functools.partial(local, mesh.shape["ctx"]) if square else general,
        mesh=mesh,
        in_specs=(
            P(("ctx", "chan"), None),
            P(None, None, "chan"),
            P(None, None, "chan"),
            P(None, "chan"),
            P(None, "chan"),
            P("chan"),
            P("chan", None),
        ),
        out_specs=P(("ctx", "chan"), None),
        check_vma=False,
    )
```

```python
import functools

import jax
import jax.numpy as jnp
from jax import lax
from jax.experimental import pallas as pl
from jax.experimental.pallas import tpu as pltpu
from jax.sharding import PartitionSpec as P

MESH = pl.DeviceIdType.MESH
F32, BF16 = jnp.float32, jnp.bfloat16
LANES, SUBS, PAD = 128, 8, 8
CHAN = 8
UNROLL = 4


def kernel(
    ctxs, tokens, in_w, short_w, decay_in, residue_in, skip, out_w, out,
    grid_buf, w_buf, wo_buf, feat, excl, block_end, state, gated, gated16,
    query, driven_by, halo_in, decay, residue, load_sem, ag_send, ag_recv, halo_send, halo_recv, st_send, st_recv,
    cp_send, cp_recv, link_send, link_recv, credit, out_sem,
):
    ctx, me = lax.axis_index("ctx"), lax.axis_index("chan")
    core, xpos, ypos = me % 2, (me // 2) % 2, me // 4
    to_core, to_x, to_y = 1 - 2 * core, 2 - 4 * xpos, 4 - 8 * ypos
    cp, xp, yp = me + to_core, me + to_x, me + to_y
    diag = me + to_x + to_y
    rows, width = tokens.shape
    half = rows // 2
    tiles = in_w.shape[2] // LANES
    modes = decay_in.shape[0]
    seq_rows = rows * CHAN
    step_rows = rows // SUBS
    top, low = pl.ds(0, half), pl.ds(half, half)

    def send(src, dst, send_sem, recv_sem, chan=None, to_ctx=None):
        where = {"chan": chan} if to_ctx is None else {"ctx": to_ctx}
        return pltpu.make_async_remote_copy(
            src_ref=src, dst_ref=dst, send_sem=send_sem, recv_sem=recv_sem,
            device_id=where, device_id_type=MESH,
        )

    barrier = pltpu.get_barrier_semaphore()
    for partner in (cp, xp, yp):
        pl.semaphore_signal(barrier, inc=1, device_id={"chan": partner}, device_id_type=MESH)
    for off in range(1, ctxs):
        pl.semaphore_signal(
            barrier, inc=1, device_id={"ctx": (ctx + off) % ctxs}, device_id_type=MESH
        )

    loads = [pltpu.make_async_copy(tokens, grid_buf.at[me], load_sem.at[0])]
    loads += [
        pltpu.make_async_copy(in_w.at[j], w_buf.at[j], load_sem.at[1 + j]) for j in range(3)
    ]
    loads += [pltpu.make_async_copy(out_w, wo_buf, load_sem.at[4])]
    for load in loads:
        load.start()
    pl.semaphore_wait(barrier, 3 + ctxs - 1)

    def hop(i, block, part, to, src=None):
        src = grid_buf.at[block, part] if src is None else src
        return send(src, grid_buf.at[block, part], ag_send.at[i], ag_recv.at[i], chan=to)

    whole = pl.ds(0, rows)
    sent = [
        hop(0, me, top, xp, tokens.at[top]),
        hop(1, me, low, yp, tokens.at[low]),
        hop(2, me, whole, cp, tokens),
        hop(3, me, low, xp, tokens.at[low]),
        hop(4, me, top, yp, tokens.at[top]),
    ]
    for copy in sent:
        copy.start()

    def forward(i, block, part, to):
        copy = hop(i, block, part, to)
        copy.start()
        sent.append(copy)

    def arrived(i, block, part):
        hop(i, block, part, cp).wait_recv()

    def project(block):
        start = pl.multiple_of(PAD + block * rows, SUBS)

        def kind(j, _):
            made = jnp.dot(grid_buf[block], w_buf[j], preferred_element_type=F32)
            made = made.astype(BF16).astype(F32)
            for l in range(tiles):
                feat[j * tiles + l, pl.ds(start, rows), :] = made[:, l * LANES:(l + 1) * LANES]
            return 0

        lax.fori_loop(0, 3, kind, 0)

    def lanes_of(l):
        return pl.ds(pl.multiple_of(l * LANES, LANES), LANES)

    sub = lax.broadcasted_iota(jnp.int32, (modes, SUBS, LANES), 1)
    sub2 = lax.broadcasted_iota(jnp.int32, (SUBS, LANES), 0)
    wide = (modes, SUBS, LANES)

    def stepped(block, i):
        return pl.ds(pl.multiple_of(block * rows + i * SUBS, SUBS), SUBS)

    def first_pass(block):
        base = PAD + block * rows

        def tile(l, _):
            rate = jnp.broadcast_to(decay[:, :, lanes_of(l)], wide)
            pole = jnp.exp(-rate)
            taps = [
                [jnp.broadcast_to(short_w[k, j:j + 1, lanes_of(l)], (SUBS, LANES)) for j in range(3)]
                for k in range(3)
            ]

            def at(i):
                return pl.ds(base + i, SUBS, step_rows)

            def steps(it, carry):
                s, last, before = carry
                for u in range(UNROLL):
                    i = it * UNROLL + u
                    now = [feat[j * tiles + l, at(i), :] for j in range(3)]
                    made = [
                        taps[0][j] * now[j] + taps[1][j] * last[j] + taps[2][j] * before[j]
                        for j in range(3)
                    ]
                    driven = made[1] * made[2]
                    query[l, stepped(block, i), :] = made[0]
                    driven_by[l, stepped(block, i), :] = driven
                    s = pole * s + driven[None]
                    last, before = now, last
                return s, last, before

            there = (sub2 > 0) | (block % 2 == 1)

            def ahead(i):
                return [
                    jnp.where(there, feat[j * tiles + l, at(i), :], 0.0) for j in range(3)
                ]

            s, _, _ = lax.fori_loop(
                0, step_rows // UNROLL, steps, (jnp.zeros(wide, F32), ahead(-1), ahead(-2))
            )
            for shift in (1, 2, 4):
                fade = jnp.exp(-rate * float(step_rows * shift))
                s = s + jnp.where(sub >= shift, pltpu.roll(s, shift, 1) * fade, 0.0)
            excl[block, l] = jnp.where(sub >= 1, pltpu.roll(s, 1, 1), 0.0)
            block_end[block, l] = s[:, SUBS - 1:SUBS, :]
            return 0

        lax.fori_loop(0, tiles, tile, 0)

    def first_rows(block):
        start = PAD + block * rows
        at_start = pl.ds(pl.multiple_of(start, SUBS), SUBS)
        at_prior = pl.ds(pl.multiple_of(start - PAD, SUBS), SUBS)
        steps = (stepped(block, 0), stepped(block, 1))

        def tile(l, _):
            made = []
            for j in range(3):
                own, prior = feat[j * tiles + l, at_start, :], feat[j * tiles + l, at_prior, :]
                last = jnp.where(sub2 < 1, pltpu.roll(prior, 1, 0), pltpu.roll(own, 1, 0))
                before = jnp.where(sub2 < 2, pltpu.roll(prior, 2, 0), pltpu.roll(own, 2, 0))
                tap = [
                    jnp.broadcast_to(short_w[k, j:j + 1, lanes_of(l)], (SUBS, LANES))
                    for k in range(3)
                ]
                made.append(tap[0] * own + tap[1] * last + tap[2] * before)
            made_driven = made[1] * made[2]
            more = []
            for i, at in enumerate(steps):
                row = jnp.broadcast_to(made[0][i:i + 1, :], (SUBS, LANES))
                query[l, at, :] = jnp.where(sub2 < 1, row, query[l, at, :])
                row = jnp.broadcast_to(made_driven[i:i + 1, :], (SUBS, LANES))
                old = driven_by[l, at, :]
                driven_by[l, at, :] = jnp.where(sub2 < 1, row, old)
                more.append((row - old)[0:1, :][None])
            zeroth, first = more
            rate = decay[:, :, lanes_of(l)]
            up = jnp.exp(rate)
            lag = jnp.maximum(sub * step_rows - 1, 0).astype(F32)
            fade = jnp.exp(-jnp.broadcast_to(rate, wide) * lag)
            add = fade * (zeroth + jnp.broadcast_to(up * first, wide))
            excl[block, l] = excl[block, l] + jnp.where(sub >= 1, add, 0.0)
            block_end[block, l] = block_end[block, l] + jnp.exp(-rate * float(rows - 1)) * (
                zeroth + up * first
            )
            return 0

        lax.fori_loop(0, tiles, tile, 0)

    for r in range(modes):
        decay[r] = decay_in[r:r + 1, :]
        residue[r] = residue_in[r:r + 1, :]
    for load in loads[:4]:
        load.wait()
    project(me)
    arrived(2, cp, whole)
    project(cp)
    first_pass(me - core + 1)
    first_pass(me - core)
    arrived(0, xp, top)
    forward(5, xp, top, yp)
    forward(7, xp, top, cp)
    arrived(1, yp, low)
    forward(6, yp, low, xp)
    forward(8, yp, low, cp)
    arrived(3, xp, low)
    forward(9, xp, low, cp)
    arrived(4, yp, top)
    forward(10, yp, top, cp)
    project(xp)
    project(yp)
    arrived(7, cp + to_x, top)
    arrived(9, cp + to_x, low)
    project(cp + to_x)
    arrived(8, cp + to_y, low)
    arrived(10, cp + to_y, top)
    project(cp + to_y)
    for even in (xp - core, yp - core):
        first_pass(even + 1)
        first_pass(even)
    arrived(5, diag, top)
    forward(11, diag, top, cp)
    arrived(6, diag, low)
    forward(12, diag, low, cp)
    project(diag)
    arrived(11, diag + to_core, top)
    arrived(12, diag + to_core, low)
    project(diag + to_core)

    halo = send(
        feat.at[:, pl.ds(seq_rows, PAD)], halo_in, halo_send, halo_recv,
        to_ctx=(ctx + 1) % ctxs,
    )

    @pl.when(ctx < ctxs - 1)
    def _():
        halo.start()

    first_pass(diag - core + 1)
    first_pass(diag - core)
    for copy in sent:
        copy.wait_send()
    for partner in (cp, xp, yp):
        pl.semaphore_signal(credit, inc=1, device_id={"chan": partner}, device_id_type=MESH)

    def fix(half_block, _):
        first_rows(2 * half_block)
        return 0

    lax.fori_loop(1, CHAN // 2, fix, 0)

    @pl.when(ctx == 0)
    def _():
        feat[:, 0:PAD, :] = jnp.zeros((3 * tiles, PAD, LANES), F32)

    @pl.when(ctx > 0)
    def _():
        halo.wait_recv()
        feat[:, 0:PAD, :] = halo_in[...]

    @pl.when(ctx < ctxs - 1)
    def _():
        halo.wait_send()

    first_rows(0)

    def own_state(l, _):
        fade = jnp.exp(-decay[:, :, lanes_of(l)] * float(rows))
        total = block_end[0, l]
        for block in range(1, CHAN):
            total = fade * total + block_end[block, l]
        state[ctx, l] = total
        return 0

    lax.fori_loop(0, tiles, own_state, 0)
    state_copies = []
    for off in range(1, ctxs):
        copy = send(
            state.at[ctx], state.at[ctx], st_send.at[off], st_recv.at[off],
            to_ctx=(ctx + off) % ctxs,
        )
        copy.start()
        state_copies.append(copy)
    for off in range(1, ctxs):
        source = (ctx + ctxs - off) % ctxs
        send(
            state.at[source], state.at[source], st_send.at[off], st_recv.at[off], to_ctx=source
        ).wait_recv()

    def enter(l, _):
        rate = decay[:, :, lanes_of(l)]
        s = jnp.zeros((modes, 1, LANES), F32)
        for off in range(1, ctxs):
            source = (ctx + ctxs - off) % ctxs
            known = jnp.where(ctx >= off, 1.0, 0.0).astype(F32)
            s = s + known * jnp.exp(-rate * float(seq_rows * (off - 1))) * state[source, l]
        fade = jnp.exp(-rate * float(rows))
        inner = jnp.exp(-jnp.broadcast_to(rate, wide) * (sub * step_rows).astype(F32))
        for block in range(CHAN):
            excl[block, l] = excl[block, l] + inner * s
            s = fade * s + block_end[block, l]
        return 0

    lax.fori_loop(0, tiles, enter, 0)

    def gate(block):
        def tile(l, _):
            rate = jnp.broadcast_to(decay[:, :, lanes_of(l)], wide)
            pole = jnp.exp(-rate)
            gain = jnp.broadcast_to(residue[:, :, lanes_of(l)], wide) * jnp.sqrt(2.0 * rate)
            direct = jnp.broadcast_to(skip[:, lanes_of(l)], (SUBS, LANES))

            def steps(it, s):
                for u in range(UNROLL):
                    i = it * UNROLL + u
                    driven = driven_by[l, stepped(block, i), :]
                    s = pole * s + driven[None]
                    y = jnp.sum(gain * s, axis=0) + direct * driven
                    gated[l, pl.ds(i, SUBS, step_rows), :] = (
                        query[l, stepped(block, i), :] * y
                    )
                return s

            lax.fori_loop(0, step_rows // UNROLL, steps, excl[block, l])
            return 0

        lax.fori_loop(0, tiles, tile, 0)
        for l in range(tiles):
            gated16[:, l * LANES:(l + 1) * LANES] = gated[l].astype(BF16)

    cut = 512

    def over_width(body):
        def one(t, _):
            body(pl.ds(pl.multiple_of(t * cut, cut), cut))
            return 0

        lax.fori_loop(0, width // cut, one, 0)

    def multiply(slot, add, part=whole):
        def body(cols):
            made = jnp.dot(gated16[part, :], wo_buf[:, cols], preferred_element_type=F32).astype(BF16)
            if add:
                made = (grid_buf[slot, part, cols].astype(F32) + made.astype(F32)).astype(BF16)
            grid_buf[slot, part, cols] = made

        over_width(body)

    loads[4].wait()
    pl.semaphore_wait(credit, 3)

    def link(i, src_slot, dst_slot, part, to):
        return send(
            grid_buf.at[src_slot, part], grid_buf.at[dst_slot, part],
            link_send.at[i], link_recv.at[i], chan=to,
        )

    linked = []

    def go(*what):
        copy = link(*what)
        copy.start()
        linked.append(copy)

    to_other = []
    for i, mine in enumerate((diag, xp, yp, me)):
        stage = 7 + i % 2
        parts = ((top, 0), (low, 4)) if i == 0 else ((whole, i),)
        gate(mine + to_core)
        if i >= 2:
            for copy in to_other[i - 2]:
                copy.wait_send()
        copies = []
        for part, sem in parts:
            multiply(stage, False, part)
            copy = send(
                grid_buf.at[stage, part], grid_buf.at[i, part],
                cp_send.at[sem], cp_recv.at[sem], chan=cp,
            )
            copy.start()
            copies.append(copy)
        to_other.append(copies)
        gate(mine)
        for copy, (part, _) in zip(copies, parts):
            copy.wait_recv()
            multiply(i, True, part)
            if i == 0 and part is top:
                go(0, 0, 4, top, xp)
            if i == 0 and part is low:
                go(1, 0, 4, low, yp)
        if i == 1:
            go(2, 1, 5, top, xp)
        if i == 2:
            go(3, 2, 6, low, yp)

    def join(dst, part, *slots):
        def body(cols):
            total = grid_buf[slots[0], part, cols].astype(F32)
            for slot in slots[1:]:
                total = total + grid_buf[slot, part, cols].astype(F32)
            grid_buf[dst, part, cols] = total.astype(BF16)

        over_width(body)

    link(1, 0, 4, low, yp).wait_recv()
    join(1, low, 1, 4)
    go(4, 1, 5, low, xp)
    link(0, 0, 4, top, xp).wait_recv()
    join(2, top, 2, 4)
    go(5, 2, 6, top, yp)
    for copies in to_other[2:]:
        for copy in copies:
            copy.wait_send()
    results = []
    for h, part, early, late in ((0, top, (2, 5), (5, 6)), (1, low, (3, 6), (4, 5))):
        link(early[0], 0, early[1], part, xp).wait_recv()
        link(late[0], 0, late[1], part, xp).wait_recv()
        join(7, part, 3, 5, 6)
        result = pltpu.make_async_copy(grid_buf.at[7, part], out.at[part], out_sem.at[h])
        result.start()
        results.append(result)
    for copy in linked:
        copy.wait_send()
    for copy in state_copies:
        copy.wait_send()
    for result in results:
        result.wait()


def local(ctxs, tokens, in_weight, short_weight, decay_rate, residue, skip_gain, out_weight):
    rows, width = tokens.shape
    chans = in_weight.shape[2]
    modes = decay_rate.shape[0]
    tiles = chans // LANES
    seq_rows = rows * CHAN
    any_spec = pl.BlockSpec(memory_space=pl.ANY)
    vmem = pl.BlockSpec(memory_space=pltpu.VMEM)
    dma = pltpu.SemaphoreType.DMA
    return pl.pallas_call(
        functools.partial(kernel, ctxs),
        out_shape=jax.ShapeDtypeStruct((rows, width), BF16),
        in_specs=[any_spec, any_spec, vmem, vmem, vmem, vmem, any_spec],
        out_specs=any_spec,
        scratch_shapes=[
            pltpu.VMEM((CHAN + 1, rows, width), BF16),
            pltpu.VMEM(in_weight.shape, BF16),
            pltpu.VMEM(out_weight.shape, BF16),
            pltpu.VMEM((3 * tiles, PAD + seq_rows, LANES), F32),
            pltpu.VMEM((CHAN, tiles, modes, SUBS, LANES), F32),
            pltpu.VMEM((CHAN, tiles, modes, 1, LANES), F32),
            pltpu.VMEM((ctxs, tiles, modes, 1, LANES), F32),
            pltpu.VMEM((tiles, rows, LANES), F32),
            pltpu.VMEM((rows, chans), BF16),
            pltpu.VMEM((tiles, seq_rows, LANES), F32),
            pltpu.VMEM((tiles, seq_rows, LANES), F32),
            pltpu.VMEM((3 * tiles, PAD, LANES), F32),
            pltpu.VMEM((modes, 1, chans), F32),
            pltpu.VMEM((modes, 1, chans), F32),
            dma((5,)), dma((13,)), dma((13,)), dma, dma, dma((ctxs,)), dma((ctxs,)),
            dma((5,)), dma((5,)), dma((6,)), dma((6,)),
            pltpu.SemaphoreType.REGULAR, dma((2,)),
        ],
        compiler_params=pltpu.CompilerParams(
            collective_id=0, has_side_effects=True, vmem_limit_bytes=62 * 2**20
        ),
        cost_estimate=pl.CostEstimate(
            flops=2 * seq_rows * width * 4 * chans,
            bytes_accessed=2 * 4 * width * chans + 4 * rows * width,
            transcendentals=0,
        ),
    )(
        tokens, in_weight, short_weight,
        decay_rate, residue, skip_gain.reshape(1, chans), out_weight,
    )


HIGH = lax.Precision.HIGHEST


def from_behind(array, axis, by):
    size = lax.axis_size(axis)
    pairs = [(i, i + by) for i in range(size) if 0 <= i + by < size]
    return lax.ppermute(array, axis, pairs)


def prefix(array, axis, combine, identity):
    size, mine = (lax.axis_size(axis), lax.axis_index(axis))
    everything = jax.tree.map(
        lambda part, kind: lax.all_gather(part.astype(kind), axis),
        array,
        (jnp.bfloat16, jnp.bfloat16),
    )
    start = jax.tree.map(
        lambda part, zero: jnp.broadcast_to(jnp.asarray(zero, part.dtype), part.shape),
        array,
        identity,
    )

    def lap(k, before):
        reached = k < mine
        new = combine(
            before, jax.tree.map(lambda part, own: part[k].astype(own.dtype), everything, array)
        )
        return jax.tree.map(lambda a, b: jnp.where(reached, a, b), new, before)

    return lax.fori_loop(0, size, lap, start)


def merge_states(earlier, latter):
    return (earlier[0] * latter[0], latter[0] * earlier[1] + latter[1])


def general(tokens, in_weight, short_weight, decay_rate, residue, skip_gain, out_weight):
    group_chans = in_weight.shape[2]
    filter_taps = short_weight.shape[0]
    projected = jnp.einsum(
        "ld,jdc->ljc",
        lax.all_gather(tokens, "chan", axis=0, tiled=True),
        in_weight,
        preferred_element_type=jnp.float32,
    ).astype(jnp.bfloat16)
    seq_rows = projected.shape[0]
    earlier_rows = from_behind(projected[seq_rows - (filter_taps - 1) :], "ctx", 1)
    padded = jnp.concatenate([earlier_rows, projected], 0)
    features = jnp.zeros((seq_rows, 3, group_chans), jnp.float32)
    for offset in range(filter_taps):
        features = features + short_weight[offset] * padded[
            filter_taps - 1 - offset : filter_taps - 1 - offset + seq_rows
        ].astype(jnp.float32)
    query_part = features[:, 0]
    driven = features[:, 1] * features[:, 2]
    mode_gain = residue * jnp.sqrt(2.0 * decay_rate)
    block_len = 128
    block_count = seq_rows // block_len
    lag_steps = jnp.arange(block_len, dtype=jnp.float32)
    decay_table = jnp.exp(-decay_rate[:, None, :] * lag_steps[None, :, None])
    lag_filter = jnp.sum(decay_table * mode_gain[:, None, :], 0)
    row_idx = jnp.arange(block_len)[:, None]
    col_idx = jnp.arange(block_len)[None, :]
    lag_index = jnp.maximum(row_idx - col_idx, 0)
    toeplitz = jnp.where(
        (row_idx >= col_idx)[:, :, None], jnp.take(lag_filter, lag_index, axis=0), 0.0
    )
    blocked = driven.reshape(block_count, block_len, group_chans)
    inner_part = jnp.einsum("ijc,bjc->bic", toeplitz, blocked, precision=HIGH)
    block_ends = jnp.einsum("rjc,bjc->brc", decay_table[:, ::-1, :], blocked, precision=HIGH)
    block_pos = jnp.arange(block_count, dtype=jnp.float32)
    block_gap = block_pos[:, None] - 1.0 - block_pos[None, :]
    block_mix = jnp.where(
        (block_gap >= 0.0)[:, :, None, None],
        jnp.exp(
            -decay_rate[None, None] * block_len * jnp.maximum(block_gap, 0.0)[:, :, None, None]
        ),
        0.0,
    )
    before = jnp.einsum("xyrc,yrc->xrc", block_mix, block_ends, precision=HIGH)
    tail_weight = jnp.exp(
        -decay_rate[None] * block_len * (block_count - 1.0 - block_pos)[:, None, None]
    )
    own_state = jnp.sum(tail_weight * block_ends, 0)
    device_span = jnp.exp(-decay_rate * seq_rows)
    identity = (jnp.ones_like(device_span), jnp.zeros_like(own_state))
    entering = prefix((device_span, own_state), "ctx", merge_states, identity)[1]
    before = (
        before + jnp.exp(-decay_rate[None] * block_len * block_pos[:, None, None]) * entering[None]
    )
    rise_table = mode_gain[:, None, :] * decay_table * jnp.exp(-decay_rate)[:, None, :]
    carried = jnp.einsum("ric,brc->bic", rise_table, before, precision=HIGH)
    long_conv = (inner_part + carried).reshape(seq_rows, group_chans)
    gated = (query_part * (long_conv + skip_gain * driven)).astype(jnp.bfloat16)
    rounded = jnp.dot(gated, out_weight, preferred_element_type=jnp.float32).astype(jnp.bfloat16)
    return lax.psum_scatter(
        lax.optimization_barrier(rounded).astype(jnp.float32).astype(jnp.bfloat16),
        "chan",
        scatter_dimension=0,
        tiled=True,
    )


def solution(mesh):
    square = mesh.shape["chan"] == CHAN
    return jax.shard_map(
        functools.partial(local, mesh.shape["ctx"]) if square else general,
        mesh=mesh,
        in_specs=(
            P(("ctx", "chan"), None),
            P(None, None, "chan"),
            P(None, None, "chan"),
            P(None, "chan"),
            P(None, "chan"),
            P("chan"),
            P("chan", None),
        ),
        out_specs=P(("ctx", "chan"), None),
        check_vma=False,
    )
```

```python
import functools

import jax
import jax.numpy as jnp
from jax import lax
from jax.experimental import pallas as pl
from jax.experimental.pallas import tpu as pltpu
from jax.sharding import PartitionSpec as P

MESH = pl.DeviceIdType.MESH
F32, BF16 = jnp.float32, jnp.bfloat16
LANES, SUBS, PAD = 128, 8, 8
CHAN = 8
UNROLL = 4


def kernel(
    ctxs, tokens, in_w, short_w, decay_in, residue_in, skip, out_w, out,
    grid_buf, w_buf, wo_buf, feat, excl, block_end, state, gated, gated16,
    driven_by, halo_in, decay, residue, load_sem, ag_send, ag_recv, halo_send, halo_recv, st_send, st_recv,
    cp_send, cp_recv, link_send, link_recv, credit, out_sem,
):
    ctx, me = lax.axis_index("ctx"), lax.axis_index("chan")
    core, xpos, ypos = me % 2, (me // 2) % 2, me // 4
    to_core, to_x, to_y = 1 - 2 * core, 2 - 4 * xpos, 4 - 8 * ypos
    cp, xp, yp = me + to_core, me + to_x, me + to_y
    diag = me + to_x + to_y
    rows, width = tokens.shape
    half = rows // 2
    tiles = in_w.shape[2] // LANES
    modes = decay_in.shape[0]
    seq_rows = rows * CHAN
    step_rows = rows // SUBS
    top, low = pl.ds(0, half), pl.ds(half, half)

    def send(src, dst, send_sem, recv_sem, chan=None, to_ctx=None):
        where = {"chan": chan} if to_ctx is None else {"ctx": to_ctx}
        return pltpu.make_async_remote_copy(
            src_ref=src, dst_ref=dst, send_sem=send_sem, recv_sem=recv_sem,
            device_id=where, device_id_type=MESH,
        )

    barrier = pltpu.get_barrier_semaphore()
    for partner in (cp, xp, yp):
        pl.semaphore_signal(barrier, inc=1, device_id={"chan": partner}, device_id_type=MESH)
    for off in range(1, ctxs):
        pl.semaphore_signal(
            barrier, inc=1, device_id={"ctx": (ctx + off) % ctxs}, device_id_type=MESH
        )

    loads = [pltpu.make_async_copy(tokens, grid_buf.at[me], load_sem.at[0])]
    loads += [
        pltpu.make_async_copy(in_w.at[j], w_buf.at[j], load_sem.at[1 + j]) for j in range(3)
    ]
    loads += [pltpu.make_async_copy(out_w, wo_buf, load_sem.at[4])]
    for load in loads:
        load.start()
    pl.semaphore_wait(barrier, 3 + ctxs - 1)

    def hop(i, block, part, to, src=None):
        src = grid_buf.at[block, part] if src is None else src
        return send(src, grid_buf.at[block, part], ag_send.at[i], ag_recv.at[i], chan=to)

    whole = pl.ds(0, rows)
    sent = [
        hop(0, me, top, xp, tokens.at[top]),
        hop(1, me, low, yp, tokens.at[low]),
        hop(2, me, whole, cp, tokens),
        hop(3, me, low, xp, tokens.at[low]),
        hop(4, me, top, yp, tokens.at[top]),
    ]
    for copy in sent:
        copy.start()

    def forward(i, block, part, to):
        copy = hop(i, block, part, to)
        copy.start()
        sent.append(copy)

    def arrived(i, block, part):
        hop(i, block, part, cp).wait_recv()

    def project(block, first=0, last=3):
        start = pl.multiple_of(PAD + block * rows, SUBS)

        def kind(j, _):
            made = jnp.dot(grid_buf[block], w_buf[j], preferred_element_type=F32)
            made = made.astype(BF16).astype(F32)
            for l in range(tiles):
                feat[j * tiles + l, pl.ds(start, rows), :] = made[:, l * LANES:(l + 1) * LANES]
            return 0

        lax.fori_loop(first, last, kind, 0)

    def lanes_of(l):
        return pl.ds(pl.multiple_of(l * LANES, LANES), LANES)

    sub = lax.broadcasted_iota(jnp.int32, (modes, SUBS, LANES), 1)
    sub2 = lax.broadcasted_iota(jnp.int32, (SUBS, LANES), 0)
    wide = (modes, SUBS, LANES)

    def stepped(block, i):
        return pl.ds(pl.multiple_of(block * rows + i * SUBS, SUBS), SUBS)

    def first_pass(block):
        base = PAD + block * rows

        def tile(l, _):
            rate = jnp.broadcast_to(decay[:, :, lanes_of(l)], wide)
            pole = jnp.exp(-rate)
            taps = [
                [jnp.broadcast_to(short_w[k, j:j + 1, lanes_of(l)], (SUBS, LANES)) for j in (1, 2)]
                for k in range(3)
            ]

            def at(i):
                return pl.ds(base + i, SUBS, step_rows)

            def steps(it, carry):
                s, last, before = carry
                for u in range(UNROLL):
                    i = it * UNROLL + u
                    now = [feat[j * tiles + l, at(i), :] for j in (1, 2)]
                    made = [
                        taps[0][j] * now[j] + taps[1][j] * last[j] + taps[2][j] * before[j]
                        for j in range(2)
                    ]
                    driven = made[0] * made[1]
                    driven_by[l, stepped(block, i), :] = driven
                    s = pole * s + driven[None]
                    last, before = now, last
                return s, last, before

            there = (sub2 > 0) | (block % 2 == 1)

            def ahead(i):
                return [
                    jnp.where(there, feat[j * tiles + l, at(i), :], 0.0) for j in (1, 2)
                ]

            s, _, _ = lax.fori_loop(
                0, step_rows // UNROLL, steps, (jnp.zeros(wide, F32), ahead(-1), ahead(-2))
            )
            for shift in (1, 2, 4):
                fade = jnp.exp(-rate * float(step_rows * shift))
                s = s + jnp.where(sub >= shift, pltpu.roll(s, shift, 1) * fade, 0.0)
            excl[block, l] = jnp.where(sub >= 1, pltpu.roll(s, 1, 1), 0.0)
            block_end[block, l] = s[:, SUBS - 1:SUBS, :]
            return 0

        lax.fori_loop(0, tiles, tile, 0)

    def first_rows(block):
        start = PAD + block * rows
        at_start = pl.ds(pl.multiple_of(start, SUBS), SUBS)
        at_prior = pl.ds(pl.multiple_of(start - PAD, SUBS), SUBS)
        steps = (stepped(block, 0), stepped(block, 1))

        def tile(l, _):
            made = []
            for j in (1, 2):
                own, prior = feat[j * tiles + l, at_start, :], feat[j * tiles + l, at_prior, :]
                last = jnp.where(sub2 < 1, pltpu.roll(prior, 1, 0), pltpu.roll(own, 1, 0))
                before = jnp.where(sub2 < 2, pltpu.roll(prior, 2, 0), pltpu.roll(own, 2, 0))
                tap = [
                    jnp.broadcast_to(short_w[k, j:j + 1, lanes_of(l)], (SUBS, LANES))
                    for k in range(3)
                ]
                made.append(tap[0] * own + tap[1] * last + tap[2] * before)
            made_driven = made[0] * made[1]
            more = []
            for i, at in enumerate(steps):
                row = jnp.broadcast_to(made_driven[i:i + 1, :], (SUBS, LANES))
                old = driven_by[l, at, :]
                driven_by[l, at, :] = jnp.where(sub2 < 1, row, old)
                more.append((row - old)[0:1, :][None])
            zeroth, first = more
            rate = decay[:, :, lanes_of(l)]
            up = jnp.exp(rate)
            lag = jnp.maximum(sub * step_rows - 1, 0).astype(F32)
            fade = jnp.exp(-jnp.broadcast_to(rate, wide) * lag)
            add = fade * (zeroth + jnp.broadcast_to(up * first, wide))
            excl[block, l] = excl[block, l] + jnp.where(sub >= 1, add, 0.0)
            block_end[block, l] = block_end[block, l] + jnp.exp(-rate * float(rows - 1)) * (
                zeroth + up * first
            )
            return 0

        lax.fori_loop(0, tiles, tile, 0)

    for r in range(modes):
        decay[r] = decay_in[r:r + 1, :]
        residue[r] = residue_in[r:r + 1, :]
    for load in loads[:4]:
        load.wait()
    project(me)
    arrived(2, cp, whole)
    project(cp)
    first_pass(me - core + 1)
    first_pass(me - core)
    arrived(0, xp, top)
    forward(5, xp, top, yp)
    forward(7, xp, top, cp)
    arrived(1, yp, low)
    forward(6, yp, low, xp)
    forward(8, yp, low, cp)
    arrived(3, xp, low)
    forward(9, xp, low, cp)
    arrived(4, yp, top)
    forward(10, yp, top, cp)
    project(xp)
    project(yp)
    arrived(7, cp + to_x, top)
    arrived(9, cp + to_x, low)
    project(cp + to_x)
    arrived(8, cp + to_y, low)
    arrived(10, cp + to_y, top)
    project(cp + to_y)
    for even in (xp - core, yp - core):
        first_pass(even + 1)
        first_pass(even)
    arrived(5, diag, top)
    forward(11, diag, top, cp)
    arrived(6, diag, low)
    forward(12, diag, low, cp)
    project(diag, 1)
    arrived(11, diag + to_core, top)
    arrived(12, diag + to_core, low)
    project(diag + to_core, 1)

    def halo_of(i, kinds):
        return send(
            feat.at[kinds, pl.ds(seq_rows, PAD)], halo_in.at[kinds],
            halo_send.at[i], halo_recv.at[i], to_ctx=(ctx + 1) % ctxs,
        )

    queries, drives = pl.ds(0, tiles), pl.ds(tiles, 2 * tiles)
    halo, query_halo = halo_of(0, drives), halo_of(1, queries)

    @pl.when(ctx < ctxs - 1)
    def _():
        halo.start()

    first_pass(diag - core + 1)
    first_pass(diag - core)
    for copy in sent:
        copy.wait_send()

    def fix(half_block, _):
        first_rows(2 * half_block)
        return 0

    lax.fori_loop(1, CHAN // 2, fix, 0)

    @pl.when(ctx == 0)
    def _():
        feat[:, 0:PAD, :] = jnp.zeros((3 * tiles, PAD, LANES), F32)

    @pl.when(ctx > 0)
    def _():
        halo.wait_recv()
        feat[drives, 0:PAD, :] = halo_in[drives]

    @pl.when(ctx < ctxs - 1)
    def _():
        halo.wait_send()

    first_rows(0)

    def own_state(l, _):
        fade = jnp.exp(-decay[:, :, lanes_of(l)] * float(rows))
        total = block_end[0, l]
        for block in range(1, CHAN):
            total = fade * total + block_end[block, l]
        state[ctx, l] = total
        return 0

    lax.fori_loop(0, tiles, own_state, 0)
    state_copies = []
    for off in range(1, ctxs):
        copy = send(
            state.at[ctx], state.at[ctx], st_send.at[off], st_recv.at[off],
            to_ctx=(ctx + off) % ctxs,
        )
        copy.start()
        state_copies.append(copy)

    project(diag, 0, 1)
    project(diag + to_core, 0, 1)
    for partner in (cp, xp, yp):
        pl.semaphore_signal(credit, inc=1, device_id={"chan": partner}, device_id_type=MESH)

    @pl.when(ctx < ctxs - 1)
    def _():
        query_halo.start()

    for off in range(1, ctxs):
        source = (ctx + ctxs - off) % ctxs
        send(
            state.at[source], state.at[source], st_send.at[off], st_recv.at[off], to_ctx=source
        ).wait_recv()

    def enter(l, _):
        rate = decay[:, :, lanes_of(l)]
        s = jnp.zeros((modes, 1, LANES), F32)
        for off in range(1, ctxs):
            source = (ctx + ctxs - off) % ctxs
            known = jnp.where(ctx >= off, 1.0, 0.0).astype(F32)
            s = s + known * jnp.exp(-rate * float(seq_rows * (off - 1))) * state[source, l]
        fade = jnp.exp(-rate * float(rows))
        inner = jnp.exp(-jnp.broadcast_to(rate, wide) * (sub * step_rows).astype(F32))
        for block in range(CHAN):
            excl[block, l] = excl[block, l] + inner * s
            s = fade * s + block_end[block, l]
        return 0

    lax.fori_loop(0, tiles, enter, 0)

    @pl.when(ctx > 0)
    def _():
        query_halo.wait_recv()
        feat[queries, 0:PAD, :] = halo_in[queries]

    @pl.when(ctx < ctxs - 1)
    def _():
        query_halo.wait_send()

    def gate(block):
        def tile(l, _):
            rate = jnp.broadcast_to(decay[:, :, lanes_of(l)], wide)
            pole = jnp.exp(-rate)
            gain = jnp.broadcast_to(residue[:, :, lanes_of(l)], wide) * jnp.sqrt(2.0 * rate)
            direct = jnp.broadcast_to(skip[:, lanes_of(l)], (SUBS, LANES))

            def steps(it, s):
                for u in range(UNROLL):
                    i = it * UNROLL + u
                    driven = driven_by[l, stepped(block, i), :]
                    s = pole * s + driven[None]
                    y = jnp.sum(gain * s, axis=0) + direct * driven
                    gated[l, pl.ds(i, SUBS, step_rows), :] = y
                return s

            lax.fori_loop(0, step_rows // UNROLL, steps, excl[block, l])
            query = sum(
                short_w[k, 0:1, lanes_of(l)] * feat[l, pl.ds(PAD + block * rows - k, rows), :]
                for k in range(3)
            )
            gated[l] = query * gated[l]
            return 0

        lax.fori_loop(0, tiles, tile, 0)
        for l in range(tiles):
            gated16[:, l * LANES:(l + 1) * LANES] = gated[l].astype(BF16)

    cut = 512

    def over_width(body):
        def one(t, _):
            body(pl.ds(pl.multiple_of(t * cut, cut), cut))
            return 0

        lax.fori_loop(0, width // cut, one, 0)

    def multiply(slot, add, part=whole):
        def body(cols):
            made = jnp.dot(gated16[part, :], wo_buf[:, cols], preferred_element_type=F32).astype(BF16)
            if add:
                made = (grid_buf[slot, part, cols].astype(F32) + made.astype(F32)).astype(BF16)
            grid_buf[slot, part, cols] = made

        over_width(body)

    loads[4].wait()
    pl.semaphore_wait(credit, 3)

    def link(i, src_slot, dst_slot, part, to):
        return send(
            grid_buf.at[src_slot, part], grid_buf.at[dst_slot, part],
            link_send.at[i], link_recv.at[i], chan=to,
        )

    linked = []

    def go(*what):
        copy = link(*what)
        copy.start()
        linked.append(copy)

    to_other = []
    for i, mine in enumerate((diag, xp, yp, me)):
        stage = 7 + i % 2
        parts = ((top, 0), (low, 4)) if i == 0 else ((whole, i),)
        gate(mine + to_core)
        if i >= 2:
            for copy in to_other[i - 2]:
                copy.wait_send()
        copies = []
        for part, sem in parts:
            multiply(stage, False, part)
            copy = send(
                grid_buf.at[stage, part], grid_buf.at[i, part],
                cp_send.at[sem], cp_recv.at[sem], chan=cp,
            )
            copy.start()
            copies.append(copy)
        to_other.append(copies)
        gate(mine)
        for copy, (part, _) in zip(copies, parts):
            copy.wait_recv()
            multiply(i, True, part)
            if i == 0 and part is top:
                go(0, 0, 4, top, xp)
            if i == 0 and part is low:
                go(1, 0, 4, low, yp)
        if i == 1:
            go(2, 1, 5, top, xp)
        if i == 2:
            go(3, 2, 6, low, yp)

    def join(dst, part, *slots):
        def body(cols):
            total = grid_buf[slots[0], part, cols].astype(F32)
            for slot in slots[1:]:
                total = total + grid_buf[slot, part, cols].astype(F32)
            grid_buf[dst, part, cols] = total.astype(BF16)

        over_width(body)

    link(1, 0, 4, low, yp).wait_recv()
    join(1, low, 1, 4)
    go(4, 1, 5, low, xp)
    link(0, 0, 4, top, xp).wait_recv()
    join(2, top, 2, 4)
    go(5, 2, 6, top, yp)
    for copies in to_other[2:]:
        for copy in copies:
            copy.wait_send()
    results = []
    for h, part, early, late in ((0, top, (2, 5), (5, 6)), (1, low, (3, 6), (4, 5))):
        link(early[0], 0, early[1], part, xp).wait_recv()
        link(late[0], 0, late[1], part, xp).wait_recv()
        join(7, part, 3, 5, 6)
        result = pltpu.make_async_copy(grid_buf.at[7, part], out.at[part], out_sem.at[h])
        result.start()
        results.append(result)
    for copy in linked:
        copy.wait_send()
    for copy in state_copies:
        copy.wait_send()
    for result in results:
        result.wait()


def local(ctxs, tokens, in_weight, short_weight, decay_rate, residue, skip_gain, out_weight):
    rows, width = tokens.shape
    chans = in_weight.shape[2]
    modes = decay_rate.shape[0]
    tiles = chans // LANES
    seq_rows = rows * CHAN
    any_spec = pl.BlockSpec(memory_space=pl.ANY)
    vmem = pl.BlockSpec(memory_space=pltpu.VMEM)
    dma = pltpu.SemaphoreType.DMA
    return pl.pallas_call(
        functools.partial(kernel, ctxs),
        out_shape=jax.ShapeDtypeStruct((rows, width), BF16),
        in_specs=[any_spec, any_spec, vmem, vmem, vmem, vmem, any_spec],
        out_specs=any_spec,
        scratch_shapes=[
            pltpu.VMEM((CHAN + 1, rows, width), BF16),
            pltpu.VMEM(in_weight.shape, BF16),
            pltpu.VMEM(out_weight.shape, BF16),
            pltpu.VMEM((3 * tiles, PAD + seq_rows, LANES), F32),
            pltpu.VMEM((CHAN, tiles, modes, SUBS, LANES), F32),
            pltpu.VMEM((CHAN, tiles, modes, 1, LANES), F32),
            pltpu.VMEM((ctxs, tiles, modes, 1, LANES), F32),
            pltpu.VMEM((tiles, rows, LANES), F32),
            pltpu.VMEM((rows, chans), BF16),
            pltpu.VMEM((tiles, seq_rows, LANES), F32),
            pltpu.VMEM((3 * tiles, PAD, LANES), F32),
            pltpu.VMEM((modes, 1, chans), F32),
            pltpu.VMEM((modes, 1, chans), F32),
            dma((5,)), dma((13,)), dma((13,)), dma((2,)), dma((2,)), dma((ctxs,)), dma((ctxs,)),
            dma((5,)), dma((5,)), dma((6,)), dma((6,)),
            pltpu.SemaphoreType.REGULAR, dma((2,)),
        ],
        compiler_params=pltpu.CompilerParams(
            collective_id=0, has_side_effects=True, vmem_limit_bytes=62 * 2**20
        ),
        cost_estimate=pl.CostEstimate(
            flops=2 * seq_rows * width * 4 * chans,
            bytes_accessed=2 * 4 * width * chans + 4 * rows * width,
            transcendentals=0,
        ),
    )(
        tokens, in_weight, short_weight,
        decay_rate, residue, skip_gain.reshape(1, chans), out_weight,
    )


HIGH = lax.Precision.HIGHEST


def from_behind(array, axis, by):
    size = lax.axis_size(axis)
    pairs = [(i, i + by) for i in range(size) if 0 <= i + by < size]
    return lax.ppermute(array, axis, pairs)


def prefix(array, axis, combine, identity):
    size, mine = (lax.axis_size(axis), lax.axis_index(axis))
    everything = jax.tree.map(
        lambda part, kind: lax.all_gather(part.astype(kind), axis),
        array,
        (jnp.bfloat16, jnp.bfloat16),
    )
    start = jax.tree.map(
        lambda part, zero: jnp.broadcast_to(jnp.asarray(zero, part.dtype), part.shape),
        array,
        identity,
    )

    def lap(k, before):
        reached = k < mine
        new = combine(
            before, jax.tree.map(lambda part, own: part[k].astype(own.dtype), everything, array)
        )
        return jax.tree.map(lambda a, b: jnp.where(reached, a, b), new, before)

    return lax.fori_loop(0, size, lap, start)


def merge_states(earlier, latter):
    return (earlier[0] * latter[0], latter[0] * earlier[1] + latter[1])


def general(tokens, in_weight, short_weight, decay_rate, residue, skip_gain, out_weight):
    group_chans = in_weight.shape[2]
    filter_taps = short_weight.shape[0]
    projected = jnp.einsum(
        "ld,jdc->ljc",
        lax.all_gather(tokens, "chan", axis=0, tiled=True),
        in_weight,
        preferred_element_type=jnp.float32,
    ).astype(jnp.bfloat16)
    seq_rows = projected.shape[0]
    earlier_rows = from_behind(projected[seq_rows - (filter_taps - 1) :], "ctx", 1)
    padded = jnp.concatenate([earlier_rows, projected], 0)
    features = jnp.zeros((seq_rows, 3, group_chans), jnp.float32)
    for offset in range(filter_taps):
        features = features + short_weight[offset] * padded[
            filter_taps - 1 - offset : filter_taps - 1 - offset + seq_rows
        ].astype(jnp.float32)
    query_part = features[:, 0]
    driven = features[:, 1] * features[:, 2]
    mode_gain = residue * jnp.sqrt(2.0 * decay_rate)
    block_len = 128
    block_count = seq_rows // block_len
    lag_steps = jnp.arange(block_len, dtype=jnp.float32)
    decay_table = jnp.exp(-decay_rate[:, None, :] * lag_steps[None, :, None])
    lag_filter = jnp.sum(decay_table * mode_gain[:, None, :], 0)
    row_idx = jnp.arange(block_len)[:, None]
    col_idx = jnp.arange(block_len)[None, :]
    lag_index = jnp.maximum(row_idx - col_idx, 0)
    toeplitz = jnp.where(
        (row_idx >= col_idx)[:, :, None], jnp.take(lag_filter, lag_index, axis=0), 0.0
    )
    blocked = driven.reshape(block_count, block_len, group_chans)
    inner_part = jnp.einsum("ijc,bjc->bic", toeplitz, blocked, precision=HIGH)
    block_ends = jnp.einsum("rjc,bjc->brc", decay_table[:, ::-1, :], blocked, precision=HIGH)
    block_pos = jnp.arange(block_count, dtype=jnp.float32)
    block_gap = block_pos[:, None] - 1.0 - block_pos[None, :]
    block_mix = jnp.where(
        (block_gap >= 0.0)[:, :, None, None],
        jnp.exp(
            -decay_rate[None, None] * block_len * jnp.maximum(block_gap, 0.0)[:, :, None, None]
        ),
        0.0,
    )
    before = jnp.einsum("xyrc,yrc->xrc", block_mix, block_ends, precision=HIGH)
    tail_weight = jnp.exp(
        -decay_rate[None] * block_len * (block_count - 1.0 - block_pos)[:, None, None]
    )
    own_state = jnp.sum(tail_weight * block_ends, 0)
    device_span = jnp.exp(-decay_rate * seq_rows)
    identity = (jnp.ones_like(device_span), jnp.zeros_like(own_state))
    entering = prefix((device_span, own_state), "ctx", merge_states, identity)[1]
    before = (
        before + jnp.exp(-decay_rate[None] * block_len * block_pos[:, None, None]) * entering[None]
    )
    rise_table = mode_gain[:, None, :] * decay_table * jnp.exp(-decay_rate)[:, None, :]
    carried = jnp.einsum("ric,brc->bic", rise_table, before, precision=HIGH)
    long_conv = (inner_part + carried).reshape(seq_rows, group_chans)
    gated = (query_part * (long_conv + skip_gain * driven)).astype(jnp.bfloat16)
    rounded = jnp.dot(gated, out_weight, preferred_element_type=jnp.float32).astype(jnp.bfloat16)
    return lax.psum_scatter(
        lax.optimization_barrier(rounded).astype(jnp.float32).astype(jnp.bfloat16),
        "chan",
        scatter_dimension=0,
        tiled=True,
    )


def solution(mesh):
    square = mesh.shape["chan"] == CHAN
    return jax.shard_map(
        functools.partial(local, mesh.shape["ctx"]) if square else general,
        mesh=mesh,
        in_specs=(
            P(("ctx", "chan"), None),
            P(None, None, "chan"),
            P(None, None, "chan"),
            P(None, "chan"),
            P(None, "chan"),
            P("chan"),
            P("chan", None),
        ),
        out_specs=P(("ctx", "chan"), None),
        check_vma=False,
    )
```

```python
import functools

import jax
import jax.numpy as jnp
from jax import lax
from jax.experimental import pallas as pl
from jax.experimental.pallas import tpu as pltpu
from jax.sharding import PartitionSpec as P

MESH = pl.DeviceIdType.MESH
F32, BF16 = jnp.float32, jnp.bfloat16
LANES, SUBS, PAD = 128, 8, 8
CHAN = 8
UNROLL = 4


def kernel(
    ctxs, tokens, in_w, short_w, decay_in, residue_in, skip, out_w, out,
    grid_buf, w_buf, wo_buf, feat, excl, block_end, state, gated, gated16,
    driven_by, halo_in, decay, residue, load_sem, ag_send, ag_recv, halo_send, halo_recv, st_send, st_recv,
    cp_send, cp_recv, link_send, link_recv, credit, out_sem,
):
    ctx, me = lax.axis_index("ctx"), lax.axis_index("chan")
    core, xpos, ypos = me % 2, (me // 2) % 2, me // 4
    to_core, to_x, to_y = 1 - 2 * core, 2 - 4 * xpos, 4 - 8 * ypos
    cp, xp, yp = me + to_core, me + to_x, me + to_y
    diag = me + to_x + to_y
    rows, width = tokens.shape
    half = rows // 2
    tiles = in_w.shape[2] // LANES
    modes = decay_in.shape[0]
    seq_rows = rows * CHAN
    step_rows = rows // SUBS
    top, low = pl.ds(0, half), pl.ds(half, half)

    def send(src, dst, send_sem, recv_sem, chan=None, to_ctx=None):
        where = {"chan": chan} if to_ctx is None else {"ctx": to_ctx}
        return pltpu.make_async_remote_copy(
            src_ref=src, dst_ref=dst, send_sem=send_sem, recv_sem=recv_sem,
            device_id=where, device_id_type=MESH,
        )

    barrier = pltpu.get_barrier_semaphore()
    for partner in (cp, xp, yp):
        pl.semaphore_signal(barrier, inc=1, device_id={"chan": partner}, device_id_type=MESH)
    for off in range(1, ctxs):
        pl.semaphore_signal(
            barrier, inc=1, device_id={"ctx": (ctx + off) % ctxs}, device_id_type=MESH
        )

    loads = [pltpu.make_async_copy(tokens, grid_buf.at[me], load_sem.at[0])]
    loads += [
        pltpu.make_async_copy(in_w.at[j], w_buf.at[j], load_sem.at[1 + j]) for j in range(3)
    ]
    loads += [pltpu.make_async_copy(out_w, wo_buf, load_sem.at[4])]
    for load in loads:
        load.start()
    pl.semaphore_wait(barrier, 3 + ctxs - 1)

    def hop(i, block, part, to, src=None):
        src = grid_buf.at[block, part] if src is None else src
        return send(src, grid_buf.at[block, part], ag_send.at[i], ag_recv.at[i], chan=to)

    whole = pl.ds(0, rows)
    sent = [
        hop(0, me, top, xp, tokens.at[top]),
        hop(1, me, low, yp, tokens.at[low]),
        hop(2, me, whole, cp, tokens),
        hop(3, me, low, xp, tokens.at[low]),
        hop(4, me, top, yp, tokens.at[top]),
    ]
    for copy in sent:
        copy.start()

    def forward(i, block, part, to):
        copy = hop(i, block, part, to)
        copy.start()
        sent.append(copy)

    def arrived(i, block, part):
        hop(i, block, part, cp).wait_recv()

    def project(block, first=0, last=3):
        start = pl.multiple_of(PAD + block * rows, SUBS)

        def kind(j, _):
            made = jnp.dot(grid_buf[block], w_buf[j], preferred_element_type=F32)
            made = made.astype(BF16).astype(F32)
            for l in range(tiles):
                feat[j * tiles + l, pl.ds(start, rows), :] = made[:, l * LANES:(l + 1) * LANES]
            return 0

        lax.fori_loop(first, last, kind, 0)

    def lanes_of(l):
        return pl.ds(pl.multiple_of(l * LANES, LANES), LANES)

    sub = lax.broadcasted_iota(jnp.int32, (modes, SUBS, LANES), 1)
    sub2 = lax.broadcasted_iota(jnp.int32, (SUBS, LANES), 0)
    wide = (modes, SUBS, LANES)

    def stepped(block, i):
        return pl.ds(pl.multiple_of(block * rows + i * SUBS, SUBS), SUBS)

    def first_pass(block):
        base = PAD + block * rows

        def tile(l, _):
            rate = jnp.broadcast_to(decay[:, :, lanes_of(l)], wide)
            pole = jnp.exp(-rate)
            taps = [
                [jnp.broadcast_to(short_w[k, j:j + 1, lanes_of(l)], (SUBS, LANES)) for j in (1, 2)]
                for k in range(3)
            ]

            def at(i):
                return pl.ds(base + i, SUBS, step_rows)

            def steps(it, carry):
                s, last, before = carry
                for u in range(UNROLL):
                    i = it * UNROLL + u
                    now = [feat[j * tiles + l, at(i), :] for j in (1, 2)]
                    made = [
                        taps[0][j] * now[j] + taps[1][j] * last[j] + taps[2][j] * before[j]
                        for j in range(2)
                    ]
                    driven = made[0] * made[1]
                    driven_by[l, stepped(block, i), :] = driven
                    s = pole * s + driven[None]
                    last, before = now, last
                return s, last, before

            there = (sub2 > 0) | (block % 2 == 1)

            def ahead(i):
                return [
                    jnp.where(there, feat[j * tiles + l, at(i), :], 0.0) for j in (1, 2)
                ]

            s, _, _ = lax.fori_loop(
                0, step_rows // UNROLL, steps, (jnp.zeros(wide, F32), ahead(-1), ahead(-2))
            )
            for shift in (1, 2, 4):
                fade = jnp.exp(-rate * float(step_rows * shift))
                s = s + jnp.where(sub >= shift, pltpu.roll(s, shift, 1) * fade, 0.0)
            excl[block, l] = jnp.where(sub >= 1, pltpu.roll(s, 1, 1), 0.0)
            block_end[block, l] = s[:, SUBS - 1:SUBS, :]
            return 0

        lax.fori_loop(0, tiles, tile, 0)

    def first_rows(block):
        start = PAD + block * rows
        at_start = pl.ds(pl.multiple_of(start, SUBS), SUBS)
        at_prior = pl.ds(pl.multiple_of(start - PAD, SUBS), SUBS)
        steps = (stepped(block, 0), stepped(block, 1))

        def tile(l, _):
            made = []
            for j in (1, 2):
                own, prior = feat[j * tiles + l, at_start, :], feat[j * tiles + l, at_prior, :]
                last = jnp.where(sub2 < 1, pltpu.roll(prior, 1, 0), pltpu.roll(own, 1, 0))
                before = jnp.where(sub2 < 2, pltpu.roll(prior, 2, 0), pltpu.roll(own, 2, 0))
                tap = [
                    jnp.broadcast_to(short_w[k, j:j + 1, lanes_of(l)], (SUBS, LANES))
                    for k in range(3)
                ]
                made.append(tap[0] * own + tap[1] * last + tap[2] * before)
            made_driven = made[0] * made[1]
            more = []
            for i, at in enumerate(steps):
                row = jnp.broadcast_to(made_driven[i:i + 1, :], (SUBS, LANES))
                old = driven_by[l, at, :]
                driven_by[l, at, :] = jnp.where(sub2 < 1, row, old)
                more.append((row - old)[0:1, :][None])
            zeroth, first = more
            rate = decay[:, :, lanes_of(l)]
            up = jnp.exp(rate)
            lag = jnp.maximum(sub * step_rows - 1, 0).astype(F32)
            fade = jnp.exp(-jnp.broadcast_to(rate, wide) * lag)
            add = fade * (zeroth + jnp.broadcast_to(up * first, wide))
            excl[block, l] = excl[block, l] + jnp.where(sub >= 1, add, 0.0)
            block_end[block, l] = block_end[block, l] + jnp.exp(-rate * float(rows - 1)) * (
                zeroth + up * first
            )
            return 0

        lax.fori_loop(0, tiles, tile, 0)

    for r in range(modes):
        decay[r] = decay_in[r:r + 1, :]
        residue[r] = residue_in[r:r + 1, :]
    for load in loads[:4]:
        load.wait()
    project(me)
    arrived(2, cp, whole)
    project(cp)
    first_pass(me - core + 1)
    first_pass(me - core)
    arrived(0, xp, top)
    forward(5, xp, top, yp)
    forward(7, xp, top, cp)
    arrived(1, yp, low)
    forward(6, yp, low, xp)
    forward(8, yp, low, cp)
    arrived(3, xp, low)
    forward(9, xp, low, cp)
    arrived(4, yp, top)
    forward(10, yp, top, cp)
    project(xp)
    project(yp)
    arrived(7, cp + to_x, top)
    arrived(9, cp + to_x, low)
    project(cp + to_x)
    arrived(8, cp + to_y, low)
    arrived(10, cp + to_y, top)
    project(cp + to_y)
    first_pass(xp - core + 1)
    first_pass(xp - core)
    first_pass(yp - core + 1)
    arrived(5, diag, top)
    forward(11, diag, top, cp)
    arrived(6, diag, low)
    forward(12, diag, low, cp)
    project(diag, 1)
    first_pass(yp - core)
    arrived(11, diag + to_core, top)
    arrived(12, diag + to_core, low)
    project(diag + to_core, 1)

    def halo_of(i, kinds):
        return send(
            feat.at[kinds, pl.ds(seq_rows, PAD)], halo_in.at[kinds],
            halo_send.at[i], halo_recv.at[i], to_ctx=(ctx + 1) % ctxs,
        )

    queries, drives = pl.ds(0, tiles), pl.ds(tiles, 2 * tiles)
    halo, query_halo = halo_of(0, drives), halo_of(1, queries)

    @pl.when(ctx < ctxs - 1)
    def _():
        halo.start()

    first_pass(diag - core + 1)
    first_pass(diag - core)
    for copy in sent:
        copy.wait_send()

    def fix(half_block, _):
        first_rows(2 * half_block)
        return 0

    lax.fori_loop(1, CHAN // 2, fix, 0)

    @pl.when(ctx == 0)
    def _():
        feat[:, 0:PAD, :] = jnp.zeros((3 * tiles, PAD, LANES), F32)

    @pl.when(ctx > 0)
    def _():
        halo.wait_recv()
        feat[drives, 0:PAD, :] = halo_in[drives]

    @pl.when(ctx < ctxs - 1)
    def _():
        halo.wait_send()

    first_rows(0)

    def own_state(l, _):
        fade = jnp.exp(-decay[:, :, lanes_of(l)] * float(rows))
        total = block_end[0, l]
        for block in range(1, CHAN):
            total = fade * total + block_end[block, l]
        state[ctx, l] = total
        return 0

    lax.fori_loop(0, tiles, own_state, 0)
    state_copies = []
    for off in range(1, ctxs):
        copy = send(
            state.at[ctx], state.at[ctx], st_send.at[off], st_recv.at[off],
            to_ctx=(ctx + off) % ctxs,
        )
        copy.start()
        state_copies.append(copy)

    project(diag, 0, 1)
    project(diag + to_core, 0, 1)
    for partner in (cp, xp, yp):
        pl.semaphore_signal(credit, inc=1, device_id={"chan": partner}, device_id_type=MESH)

    @pl.when(ctx < ctxs - 1)
    def _():
        query_halo.start()

    for off in range(1, ctxs):
        source = (ctx + ctxs - off) % ctxs
        send(
            state.at[source], state.at[source], st_send.at[off], st_recv.at[off], to_ctx=source
        ).wait_recv()

    def enter(l, _):
        rate = decay[:, :, lanes_of(l)]
        s = jnp.zeros((modes, 1, LANES), F32)
        for off in range(1, ctxs):
            source = (ctx + ctxs - off) % ctxs
            known = jnp.where(ctx >= off, 1.0, 0.0).astype(F32)
            s = s + known * jnp.exp(-rate * float(seq_rows * (off - 1))) * state[source, l]
        fade = jnp.exp(-rate * float(rows))
        inner = jnp.exp(-jnp.broadcast_to(rate, wide) * (sub * step_rows).astype(F32))
        for block in range(CHAN):
            excl[block, l] = excl[block, l] + inner * s
            s = fade * s + block_end[block, l]
        return 0

    lax.fori_loop(0, tiles, enter, 0)

    @pl.when(ctx > 0)
    def _():
        query_halo.wait_recv()
        feat[queries, 0:PAD, :] = halo_in[queries]

    @pl.when(ctx < ctxs - 1)
    def _():
        query_halo.wait_send()

    def gate(block):
        def tile(l, _):
            rate = jnp.broadcast_to(decay[:, :, lanes_of(l)], wide)
            pole = jnp.exp(-rate)
            gain = jnp.broadcast_to(residue[:, :, lanes_of(l)], wide) * jnp.sqrt(2.0 * rate)
            direct = jnp.broadcast_to(skip[:, lanes_of(l)], (SUBS, LANES))

            def steps(it, s):
                for u in range(UNROLL):
                    i = it * UNROLL + u
                    driven = driven_by[l, stepped(block, i), :]
                    s = pole * s + driven[None]
                    y = jnp.sum(gain * s, axis=0) + direct * driven
                    gated[l, pl.ds(i, SUBS, step_rows), :] = y
                return s

            lax.fori_loop(0, step_rows // UNROLL, steps, excl[block, l])
            query = sum(
                short_w[k, 0:1, lanes_of(l)] * feat[l, pl.ds(PAD + block * rows - k, rows), :]
                for k in range(3)
            )
            gated[l] = query * gated[l]
            return 0

        lax.fori_loop(0, tiles, tile, 0)
        for l in range(tiles):
            gated16[:, l * LANES:(l + 1) * LANES] = gated[l].astype(BF16)

    cut = 512

    def over_width(body):
        def one(t, _):
            body(pl.ds(pl.multiple_of(t * cut, cut), cut))
            return 0

        lax.fori_loop(0, width // cut, one, 0)

    def multiply(slot, add, part=whole):
        def body(cols):
            made = jnp.dot(gated16[part, :], wo_buf[:, cols], preferred_element_type=F32).astype(BF16)
            if add:
                made = (grid_buf[slot, part, cols].astype(F32) + made.astype(F32)).astype(BF16)
            grid_buf[slot, part, cols] = made

        over_width(body)

    loads[4].wait()
    pl.semaphore_wait(credit, 3)

    def link(i, src_slot, dst_slot, part, to):
        return send(
            grid_buf.at[src_slot, part], grid_buf.at[dst_slot, part],
            link_send.at[i], link_recv.at[i], chan=to,
        )

    linked = []

    def go(*what):
        copy = link(*what)
        copy.start()
        linked.append(copy)

    to_other = []
    for i, mine in enumerate((diag, xp, yp, me)):
        stage = 7 + i % 2
        parts = ((top, 0), (low, 4)) if i == 0 else ((whole, i),)
        gate(mine + to_core)
        if i >= 2:
            for copy in to_other[i - 2]:
                copy.wait_send()
        copies = []
        for part, sem in parts:
            multiply(stage, False, part)
            copy = send(
                grid_buf.at[stage, part], grid_buf.at[i, part],
                cp_send.at[sem], cp_recv.at[sem], chan=cp,
            )
            copy.start()
            copies.append(copy)
        to_other.append(copies)
        gate(mine)
        for copy, (part, _) in zip(copies, parts):
            copy.wait_recv()
            multiply(i, True, part)
            if i == 0 and part is top:
                go(0, 0, 4, top, xp)
            if i == 0 and part is low:
                go(1, 0, 4, low, yp)
        if i == 1:
            go(2, 1, 5, top, xp)
        if i == 2:
            go(3, 2, 6, low, yp)

    def join(dst, part, *slots):
        def body(cols):
            total = grid_buf[slots[0], part, cols].astype(F32)
            for slot in slots[1:]:
                total = total + grid_buf[slot, part, cols].astype(F32)
            grid_buf[dst, part, cols] = total.astype(BF16)

        over_width(body)

    link(1, 0, 4, low, yp).wait_recv()
    join(1, low, 1, 4)
    go(4, 1, 5, low, xp)
    link(0, 0, 4, top, xp).wait_recv()
    join(2, top, 2, 4)
    go(5, 2, 6, top, yp)
    for copies in to_other[2:]:
        for copy in copies:
            copy.wait_send()
    results = []
    for h, part, early, late in ((0, top, (2, 5), (5, 6)), (1, low, (3, 6), (4, 5))):
        link(early[0], 0, early[1], part, xp).wait_recv()
        link(late[0], 0, late[1], part, xp).wait_recv()
        join(7, part, 3, 5, 6)
        result = pltpu.make_async_copy(grid_buf.at[7, part], out.at[part], out_sem.at[h])
        result.start()
        results.append(result)
    for copy in linked:
        copy.wait_send()
    for copy in state_copies:
        copy.wait_send()
    for result in results:
        result.wait()


def local(ctxs, tokens, in_weight, short_weight, decay_rate, residue, skip_gain, out_weight):
    rows, width = tokens.shape
    chans = in_weight.shape[2]
    modes = decay_rate.shape[0]
    tiles = chans // LANES
    seq_rows = rows * CHAN
    any_spec = pl.BlockSpec(memory_space=pl.ANY)
    vmem = pl.BlockSpec(memory_space=pltpu.VMEM)
    dma = pltpu.SemaphoreType.DMA
    return pl.pallas_call(
        functools.partial(kernel, ctxs),
        out_shape=jax.ShapeDtypeStruct((rows, width), BF16),
        in_specs=[any_spec, any_spec, vmem, vmem, vmem, vmem, any_spec],
        out_specs=any_spec,
        scratch_shapes=[
            pltpu.VMEM((CHAN + 1, rows, width), BF16),
            pltpu.VMEM(in_weight.shape, BF16),
            pltpu.VMEM(out_weight.shape, BF16),
            pltpu.VMEM((3 * tiles, PAD + seq_rows, LANES), F32),
            pltpu.VMEM((CHAN, tiles, modes, SUBS, LANES), F32),
            pltpu.VMEM((CHAN, tiles, modes, 1, LANES), F32),
            pltpu.VMEM((ctxs, tiles, modes, 1, LANES), F32),
            pltpu.VMEM((tiles, rows, LANES), F32),
            pltpu.VMEM((rows, chans), BF16),
            pltpu.VMEM((tiles, seq_rows, LANES), F32),
            pltpu.VMEM((3 * tiles, PAD, LANES), F32),
            pltpu.VMEM((modes, 1, chans), F32),
            pltpu.VMEM((modes, 1, chans), F32),
            dma((5,)), dma((13,)), dma((13,)), dma((2,)), dma((2,)), dma((ctxs,)), dma((ctxs,)),
            dma((5,)), dma((5,)), dma((6,)), dma((6,)),
            pltpu.SemaphoreType.REGULAR, dma((2,)),
        ],
        compiler_params=pltpu.CompilerParams(
            collective_id=0, has_side_effects=True, vmem_limit_bytes=62 * 2**20
        ),
        cost_estimate=pl.CostEstimate(
            flops=2 * seq_rows * width * 4 * chans,
            bytes_accessed=2 * 4 * width * chans + 4 * rows * width,
            transcendentals=0,
        ),
    )(
        tokens, in_weight, short_weight,
        decay_rate, residue, skip_gain.reshape(1, chans), out_weight,
    )


HIGH = lax.Precision.HIGHEST


def from_behind(array, axis, by):
    size = lax.axis_size(axis)
    pairs = [(i, i + by) for i in range(size) if 0 <= i + by < size]
    return lax.ppermute(array, axis, pairs)


def prefix(array, axis, combine, identity):
    size, mine = (lax.axis_size(axis), lax.axis_index(axis))
    everything = jax.tree.map(
        lambda part, kind: lax.all_gather(part.astype(kind), axis),
        array,
        (jnp.bfloat16, jnp.bfloat16),
    )
    start = jax.tree.map(
        lambda part, zero: jnp.broadcast_to(jnp.asarray(zero, part.dtype), part.shape),
        array,
        identity,
    )

    def lap(k, before):
        reached = k < mine
        new = combine(
            before, jax.tree.map(lambda part, own: part[k].astype(own.dtype), everything, array)
        )
        return jax.tree.map(lambda a, b: jnp.where(reached, a, b), new, before)

    return lax.fori_loop(0, size, lap, start)


def merge_states(earlier, latter):
    return (earlier[0] * latter[0], latter[0] * earlier[1] + latter[1])


def general(tokens, in_weight, short_weight, decay_rate, residue, skip_gain, out_weight):
    group_chans = in_weight.shape[2]
    filter_taps = short_weight.shape[0]
    projected = jnp.einsum(
        "ld,jdc->ljc",
        lax.all_gather(tokens, "chan", axis=0, tiled=True),
        in_weight,
        preferred_element_type=jnp.float32,
    ).astype(jnp.bfloat16)
    seq_rows = projected.shape[0]
    earlier_rows = from_behind(projected[seq_rows - (filter_taps - 1) :], "ctx", 1)
    padded = jnp.concatenate([earlier_rows, projected], 0)
    features = jnp.zeros((seq_rows, 3, group_chans), jnp.float32)
    for offset in range(filter_taps):
        features = features + short_weight[offset] * padded[
            filter_taps - 1 - offset : filter_taps - 1 - offset + seq_rows
        ].astype(jnp.float32)
    query_part = features[:, 0]
    driven = features[:, 1] * features[:, 2]
    mode_gain = residue * jnp.sqrt(2.0 * decay_rate)
    block_len = 128
    block_count = seq_rows // block_len
    lag_steps = jnp.arange(block_len, dtype=jnp.float32)
    decay_table = jnp.exp(-decay_rate[:, None, :] * lag_steps[None, :, None])
    lag_filter = jnp.sum(decay_table * mode_gain[:, None, :], 0)
    row_idx = jnp.arange(block_len)[:, None]
    col_idx = jnp.arange(block_len)[None, :]
    lag_index = jnp.maximum(row_idx - col_idx, 0)
    toeplitz = jnp.where(
        (row_idx >= col_idx)[:, :, None], jnp.take(lag_filter, lag_index, axis=0), 0.0
    )
    blocked = driven.reshape(block_count, block_len, group_chans)
    inner_part = jnp.einsum("ijc,bjc->bic", toeplitz, blocked, precision=HIGH)
    block_ends = jnp.einsum("rjc,bjc->brc", decay_table[:, ::-1, :], blocked, precision=HIGH)
    block_pos = jnp.arange(block_count, dtype=jnp.float32)
    block_gap = block_pos[:, None] - 1.0 - block_pos[None, :]
    block_mix = jnp.where(
        (block_gap >= 0.0)[:, :, None, None],
        jnp.exp(
            -decay_rate[None, None] * block_len * jnp.maximum(block_gap, 0.0)[:, :, None, None]
        ),
        0.0,
    )
    before = jnp.einsum("xyrc,yrc->xrc", block_mix, block_ends, precision=HIGH)
    tail_weight = jnp.exp(
        -decay_rate[None] * block_len * (block_count - 1.0 - block_pos)[:, None, None]
    )
    own_state = jnp.sum(tail_weight * block_ends, 0)
    device_span = jnp.exp(-decay_rate * seq_rows)
    identity = (jnp.ones_like(device_span), jnp.zeros_like(own_state))
    entering = prefix((device_span, own_state), "ctx", merge_states, identity)[1]
    before = (
        before + jnp.exp(-decay_rate[None] * block_len * block_pos[:, None, None]) * entering[None]
    )
    rise_table = mode_gain[:, None, :] * decay_table * jnp.exp(-decay_rate)[:, None, :]
    carried = jnp.einsum("ric,brc->bic", rise_table, before, precision=HIGH)
    long_conv = (inner_part + carried).reshape(seq_rows, group_chans)
    gated = (query_part * (long_conv + skip_gain * driven)).astype(jnp.bfloat16)
    rounded = jnp.dot(gated, out_weight, preferred_element_type=jnp.float32).astype(jnp.bfloat16)
    return lax.psum_scatter(
        lax.optimization_barrier(rounded).astype(jnp.float32).astype(jnp.bfloat16),
        "chan",
        scatter_dimension=0,
        tiled=True,
    )


def solution(mesh):
    square = mesh.shape["chan"] == CHAN
    return jax.shard_map(
        functools.partial(local, mesh.shape["ctx"]) if square else general,
        mesh=mesh,
        in_specs=(
            P(("ctx", "chan"), None),
            P(None, None, "chan"),
            P(None, None, "chan"),
            P(None, "chan"),
            P(None, "chan"),
            P("chan"),
            P("chan", None),
        ),
        out_specs=P(("ctx", "chan"), None),
        check_vma=False,
    )
```
